1024 devices in a mesh: outer: 64 (over z_lo, x, core), inner: 16 (over y, z_hi).
Axes of the slice: x: 4, y: 4, z: 32 (z_hi: 4, z_lo: 8; z = z_hi * 8 + z_lo), core: 2. Of those that a mesh axis runs over, the one named last changes fastest.
Arguments:
- hidden: bfloat16 [245760, 7168], P(('outer', 'inner')), may hold values from -24 to 24
- segment_ids: int32 [1024, 240], P(('outer', 'inner')), may hold values from 0 to 59, never falling along the last dimension, each value on 1 to 120 neighbouring positions
- key_grad: bfloat16 [245760, 64], P(('outer', 'inner')), may hold values from -0.024169922 to 0.024169922
- weight_bf16: bfloat16 [7168, 64], replicated, may hold values from -0.75 to 0.75
- gain_bf16: bfloat16 [7168], replicated, may hold values from 0.099609375 to 1.8984375
- weight_master: float32 [7168, 64], P(('outer', 'inner')), may hold values from -0.018 to 0.018
- weight_first: float32 [7168, 64], P(('outer', 'inner')), may hold values from -6 to 6
- weight_second: float32 [7168, 64], P(('outer', 'inner')), may hold values from 0.1 to 10
- gain_master: float32 [7168], P(('outer', 'inner')), may hold values from 0.1 to 1.9
- gain_first: float32 [7168], P(('outer', 'inner')), may hold values from -6 to 6
- gain_second: float32 [7168], P(('outer', 'inner')), may hold values from 0.1 to 10
Outputs:
- weight_master_new: float32 [7168, 64], P(('outer', 'inner'))
- weight_first_new: float32 [7168, 64], P(('outer', 'inner'))
- weight_second_new: float32 [7168, 64], P(('outer', 'inner'))
- gain_master_new: float32 [7168], P(('outer', 'inner'))
- gain_first_new: float32 [7168], P(('outer', 'inner'))
- gain_second_new: float32 [7168], P(('outer', 'inner'))
- weight_bf16_new: bfloat16 [7168, 64], replicated
- gain_bf16_new: bfloat16 [7168], replicated
The draws below stay inside these ranges and needn't reach their ends.
Inputs may be any that keep to these rules, and one draw needn't show every extreme that they name: `segment_ids`: in each row the ids never fall; each segment spans 1 to 120 tokens, one exactly that many.
All inputs are finite; a program needn't handle non-finite values.
Results may differ from the reference program's by a relative error of at most 0.0055.
Values may be sent and summed in bfloat16 or wider, within the bound.
A program may use at most 32 MiB of HBM per device.

```python
import math
import jax
import jax.numpy as jnp
import numpy as np
from jax import lax

D = 7168
ROPE = 64
TOK_DEV = 240
STEP = 20
PACKS = 1024
TOKENS = 245760


def strengthened(drawn, rng, source, target, shards_of, factor):
    def block_of(axis_at):
        return (jnp.arange(drawn.shape[axis_at]) // (drawn.shape[axis_at] // shards_of)).reshape((-1,) + (1,) * (drawn.ndim - 1 - axis_at))

    first = jax.random.permutation(rng, shards_of)[block_of(target)]
    second = (block_of(target) + shards_of // 2) % shards_of
    return jnp.where((block_of(source) == first) | (block_of(source) == second), factor * drawn, drawn)


def level_of(own_key, dims, split, low, largest):
    def one(axis_at, blocks):
        steps = jax.random.uniform(jax.random.fold_in(jax.random.fold_in(own_key, 6), axis_at), (blocks,), jnp.float32, low / len(split), largest / len(split))
        return jnp.repeat(jnp.exp(steps), dims[axis_at] // blocks).reshape((-1,) + (1,) * (len(dims) - axis_at - 1))

    loudness = one(*split[0])
    for cut in split[1:]:
        loudness = loudness * one(*cut)
    return loudness


def split_up(number_of, total, reach, lean):
    weights = [(1 << 20) // math.isqrt(standing ** lean) + 1 for standing in range(2, number_of + 1)]
    surplus, counts = total - reach - (number_of - 1), [1] * (number_of - 1)
    while surplus > 0:
        free = [i for i in range(number_of - 1) if counts[i] < reach]
        pool, left = sum([weights[i] for i in free]), surplus
        for i in free:
            extra = min(reach - counts[i], max(1, left * weights[i] // pool), surplus)
            counts[i] = counts[i] + extra
            surplus = surplus - extra
    return np.array([reach] + counts)


def ragged_sizes(rng, count, total, bound, skew):
    if count == 2:
        one = jax.random.randint(rng, (), max(1, total - bound), min(bound, total - 1) + 1)
        return jnp.stack([one, total - one])
    tallies = jnp.asarray(split_up(count, total, bound, skew), jnp.int32)
    couples = (count - 1) // 2
    donor, sink = tallies[1:1 + 2 * couples:2], tallies[2:2 + 2 * couples:2]
    margin = jnp.minimum(donor - 1, bound - sink)
    shifted = jax.random.randint(jax.random.fold_in(rng, 1), (couples,), 0, 1 << 20) % (margin + 1)
    tallies = tallies.at[1:1 + 2 * couples:2].set(donor - shifted).at[2:2 + 2 * couples:2].set(sink + shifted)
    return tallies[jax.random.permutation(jax.random.fold_in(rng, 2), count)]


def normal_values(stream_key, shape, spread, bound, split=(), held_as=jnp.bfloat16):
    result = jax.random.normal(stream_key, shape, jnp.float32) * spread
    if len(split) > 0:
        result = level_of(stream_key, shape, split, -0.22, 0.18) * result
    return jnp.clip(result, min=-bound, max=bound).astype(held_as)


def noise_with(own_key, shape, scale, bound, shards, heavy, kind=jnp.bfloat16):
    values = scale * jax.random.normal(own_key, shape, jnp.float32)
    if shards:
        values = values * level_of(own_key, shape, shards, -0.22, 0.18)
    return jnp.clip(strengthened(values, jax.random.fold_in(own_key, 3), *heavy), -bound, bound).astype(kind)


def setup_inputs(seed: int = 0) -> dict:
    keys = jax.random.split(jax.random.key(seed), 12)
    hidden = noise_with(keys[0], (TOKENS, D), 1.0, 24.0, ((0, 1024),), (0, 1, 1024, 6.0))
    segment_ids = jax.vmap(lambda own: jnp.searchsorted(jnp.cumsum(ragged_sizes(own, TOK_DEV // 4, TOK_DEV, TOK_DEV // 2, 2)), jnp.arange(TOK_DEV), side="right"))(jax.random.split(keys[1], PACKS)).reshape((PACKS, TOK_DEV)).astype(jnp.int32)
    key_grad = normal_values(keys[2], (TOKENS, ROPE), (2.0 / TOKENS ** 0.5), 0.024169922, ((0, 1024),))
    weight_bf16 = normal_values(keys[3], (D, ROPE), ROPE ** -0.5, 0.75)
    gain_bf16 = jnp.clip(1.0 + 0.18 * jax.random.normal(keys[4], (D,), jnp.float32), 0.099609375, 1.8984375).astype(jnp.bfloat16)
    weight_master = normal_values(keys[5], (D, ROPE), 0.003, 0.018, ((0, 1024),), jnp.float32)
    weight_first = normal_values(keys[6], (D, ROPE), 1.0, 6.0, ((0, 1024),), jnp.float32)
    weight_second = jnp.clip(jnp.exp(math.log(10.0) - 4.6051702 * jax.random.uniform(keys[7], (D, ROPE), jnp.float32) ** level_of(keys[7], (D, ROPE), ((0, 1024),), -0.2, 0.2)), 0.1, 10.0)
    gain_master = jnp.clip(1.0 + 0.18 * jax.random.normal(keys[8], (D,), jnp.float32), 0.1, 1.9)
    gain_first = normal_values(keys[9], (D,), 1.0, 6.0, ((0, 1024),), jnp.float32)
    gain_second = jnp.clip(jnp.exp(math.log(10.0) - 4.6051702 * jax.random.uniform(keys[10], (D,), jnp.float32) ** level_of(keys[10], (D,), ((0, 1024),), -0.2, 0.2)), 0.1, 10.0)
    return dict(hidden=hidden, segment_ids=segment_ids, key_grad=key_grad, weight_bf16=weight_bf16, gain_bf16=gain_bf16, weight_master=weight_master, weight_first=weight_first, weight_second=weight_second, gain_master=gain_master, gain_first=gain_first, gain_second=gain_second)


beta_one = 0.9
beta_two = 0.95
learning_rate = 0.00022
adam_epsilon = 1e-08
norm_epsilon = 1e-06

def rotate_back(gradient, segment_row):
    length = segment_row.shape[0]
    places = jnp.arange(length, dtype=jnp.int32)
    same_segment = segment_row[:, None] == segment_row[None, :]
    starts = lax.optimization_barrier(jnp.min(jnp.where(same_segment, places[None, :], length), axis=1))
    positions = (places - starts).astype(jnp.float32)
    half_width = gradient.shape[1] // 2
    frequency = 10000.0 ** (-jnp.arange(half_width, dtype=jnp.float32) / half_width)
    angles = positions[:, None] * frequency[None, :]
    cosine_table = jnp.cos(angles)
    sine_table = jnp.sin(angles)
    first_half = gradient[:, :half_width].astype(jnp.float32)
    second_half = gradient[:, half_width:].astype(jnp.float32)
    joined = jnp.concatenate([first_half * cosine_table + second_half * sine_table, second_half * cosine_table - first_half * sine_table], axis=1)
    return joined.astype(jnp.bfloat16)

def local_terms(hidden_rows, segment_row, grad_rows, weight_bf16, gain_bf16):
    hidden_float = hidden_rows.astype(jnp.float32)
    inverse_rms = lax.rsqrt(lax.optimization_barrier(jnp.mean(hidden_float * hidden_float, axis=1, keepdims=True)) + norm_epsilon)
    normed = hidden_float * inverse_rms
    scaled = (normed * gain_bf16.astype(jnp.float32)).astype(jnp.bfloat16)
    key_latent = rotate_back(grad_rows, segment_row)
    weight_grad = lax.dot_general(scaled, key_latent, (((0,), (0,)), ((), ())), preferred_element_type=jnp.float32)
    input_grad = lax.dot_general(key_latent, weight_bf16, (((1,), (1,)), ((), ())), preferred_element_type=jnp.float32)
    gain_grad = lax.optimization_barrier(jnp.sum(input_grad * normed, axis=0))
    return (weight_grad, gain_grad)

def adamw(master, first, second, gradient, decay):
    first_new = beta_one * first + (1.0 - beta_one) * gradient
    second_new = beta_two * second + (1.0 - beta_two) * gradient * gradient
    correct_one = 1.0 - beta_one ** (STEP + 1)
    correct_two = 1.0 - beta_two ** (STEP + 1)
    direction = first_new / correct_one / (jnp.sqrt(second_new / correct_two) + adam_epsilon)
    master_new = master - learning_rate * (direction + decay * master)
    return (master_new, first_new, second_new)

def reference(hidden, segment_ids, key_grad, weight_bf16, gain_bf16, weight_master, weight_first, weight_second, gain_master, gain_first, gain_second):
    hidden_rows = hidden.reshape(PACKS, TOK_DEV, D)
    grad_rows = key_grad.reshape(PACKS, TOK_DEV, ROPE)

    def accumulate(carry, pieces):
        weight_total, gain_total = carry
        weight_grad, gain_grad = local_terms(pieces[0], pieces[1], pieces[2], weight_bf16, gain_bf16)
        return ((weight_total + weight_grad, gain_total + gain_grad), None)
    start = (jnp.zeros((D, ROPE), jnp.float32), jnp.zeros((D,), jnp.float32))
    totals, unused = lax.scan(accumulate, start, (hidden_rows, segment_ids, grad_rows))
    weight_master_new, weight_first_new, weight_second_new = adamw(weight_master, weight_first, weight_second, totals[0], 0.1)
    gain_master_new, gain_first_new, gain_second_new = adamw(gain_master, gain_first, gain_second, totals[1], 0.0)
    return (weight_master_new, weight_first_new, weight_second_new, gain_master_new, gain_first_new, gain_second_new, weight_master_new.astype(jnp.bfloat16), gain_master_new.astype(jnp.bfloat16))
```

```python
import functools

import jax
import jax.numpy as jnp
import numpy as np
from jax import lax
from jax.experimental import pallas as pl
from jax.experimental.pallas import tpu as pltpu
from jax.sharding import PartitionSpec as P

STEP = 20
beta_one = 0.9
beta_two = 0.95
learning_rate = 0.00022
adam_epsilon = 1e-08
norm_epsilon = 1e-06

MESH = pl.DeviceIdType.MESH
F32 = jnp.float32
BF16 = jnp.bfloat16
ROPE = 64
HALF = ROPE // 2
OWN = 7
LANES = 128
BLOCK = OWN * LANES

NC, NX, NY, NZL, NZH = 2, 4, 4, 8, 4


def rotary_table():
    frequency = 10000.0 ** (-np.arange(HALF) / HALF)
    angles = frequency[:, None] * np.arange(LANES)[None, :]
    return np.concatenate([np.cos(angles), np.sin(angles)]).astype(np.float32)


def iota(shape, axis):
    return lax.broadcasted_iota(jnp.int32, shape, axis)


def look_up(table, index):
    rows = [
        jnp.take_along_axis(table[8 * i : 8 * i + 8], index, axis=1)
        for i in range(table.shape[0] // 8)
    ]
    return jnp.concatenate(rows, axis=0)


def pack_shard(weight_ref, gain_ref):
    gains = jnp.concatenate([gain_ref[...], jnp.zeros((1, ROPE - OWN), F32)], axis=1)
    rows = []
    for p in range(4):
        right = weight_ref[2 * p + 1 : 2 * p + 2, :] if p < 3 else gains
        rows.append(jnp.concatenate([weight_ref[2 * p : 2 * p + 1, :], right], axis=1))
    return rows


def grads_kernel(
    hidden_ref, seg_ref, key_ref, weight_ref, gain_ref, table_ref,
    wm_ref, wf_ref, ws_ref, gm_ref, gf_ref, gs_ref,
    packed_ref, shard_ref, squares, wide, segs, gains,
):
    tokens, width = hidden_ref.shape
    padded = 2 * LANES
    for a, (w, g) in enumerate(((wm_ref, gm_ref), (wf_ref, gf_ref), (ws_ref, gs_ref))):
        for p, row in enumerate(pack_shard(w, g)):
            shard_ref[4 * a + p : 4 * a + p + 1, :] = row
    shard_ref[12:16, :] = jnp.ones((4, LANES), F32)
    gains[...] = gain_ref[...].astype(F32)

    squares[tokens:, :] = jnp.zeros((padded - tokens, LANES), F32)
    step = 48

    def square(i, carry):
        rows = pl.ds(pl.multiple_of(i * step, 16), step)
        total = jnp.zeros((step, LANES), F32)
        for j in range(width // LANES):
            h = hidden_ref[rows, j * LANES : (j + 1) * LANES].astype(F32)
            total = total + h * h
        squares[rows, :] = total
        return carry

    lax.fori_loop(0, tokens // step, square, 0)
    mean = jnp.sum(squares[...].T, axis=0, keepdims=True) * (1.0 / width)
    inverse_rms = lax.rsqrt(mean + norm_epsilon)[:, :tokens]

    segs[...] = jnp.full((8, padded), -1, jnp.int32)
    segs[:, :tokens] = jnp.broadcast_to(seg_ref[...], (8, tokens))
    ids = segs[...]
    lane = iota((8, padded), 1)
    begins = jnp.logical_or(ids != pltpu.roll(ids, 1, axis=1), lane == 0)
    start = jnp.where(begins, lane, 0)
    shift = 1
    while shift < padded:
        before = pltpu.roll(start, shift, axis=1)
        start = jnp.maximum(start, jnp.where(lane >= shift, before, 0))
        shift *= 2
    place = jnp.clip(lane - start, 0, LANES - 1)
    halves = [
        look_up(table_ref[...], place[:, i * LANES : (i + 1) * LANES]) for i in range(2)
    ]
    table = jnp.concatenate(halves, axis=1)[:, :tokens]
    cosine, sine = table[:HALF], table[HALF:]
    key = key_ref[...].astype(F32)
    a, b = key[:HALF], key[HALF:]
    latent = jnp.concatenate([a * cosine + b * sine, b * cosine - a * sine], axis=0)
    latent = latent.astype(BF16).astype(F32) * inverse_rms
    high = latent.astype(BF16)
    low = (latent - high.astype(F32)).astype(BF16)
    both = jnp.concatenate([high, low], axis=0)

    row8 = iota((8, LANES), 0)
    lane8 = iota((8, LANES), 1)
    left = iota((LANES, LANES), 1) < ROPE
    upper = iota((16, 8, LANES), 1) < 4
    for k in range(width // BLOCK):
        product = jnp.dot(
            both, hidden_ref[:, k * BLOCK : (k + 1) * BLOCK], preferred_element_type=F32
        )
        product = product[:ROPE] + product[ROPE:]
        for i in range(OWN):
            at = OWN * k + i
            part = product[:, i * LANES : (i + 1) * LANES]
            w = weight_ref[:, at * LANES : (at + 1) * LANES].astype(F32)
            gain_grad = jnp.sum(w * part, axis=0, keepdims=True)
            chosen = row8 == lax.rem(lane8 + i * LANES, OWN)
            block = jnp.concatenate(
                [
                    part * gains[at : at + 1, :],
                    jnp.where(chosen, gain_grad, 0.0),
                    jnp.zeros((LANES - ROPE - 8, LANES), F32),
                ],
                axis=0,
            )
            wide[k % 2, i * LANES : (i + 1) * LANES, :] = block.T
        rows = [wide[k % 2, pl.ds(r, LANES, stride=OWN), :] for r in range(OWN)]
        total = rows[0]
        for r in range(1, OWN):
            total = total + rows[r]
        tiles = [
            jnp.where(left, rows[2 * p], pltpu.roll(rows[2 * p + 1], ROPE, axis=1))
            for p in range(3)
        ]
        tiles.append(jnp.where(left, rows[6], total))
        tiles = [t.reshape(16, 8, LANES) for t in tiles]
        even, odd = [], []
        for one, two in ((tiles[0], tiles[1]), (tiles[2], tiles[3])):
            even.append(jnp.where(upper, one, pltpu.roll(two, 4, axis=1)))
            odd.append(jnp.where(upper, pltpu.roll(one, 4, axis=1), two))
        even = jnp.concatenate(even, axis=1).astype(BF16)
        odd = jnp.concatenate(odd, axis=1).astype(BF16)
        for q in range(16):
            x, core, y = q // 4, (q // 2) % 2, 2 * (q % 2)
            packed_ref[core, x, y, k] = even[q]
            packed_ref[core, x, y + 1, k] = odd[q]


def adamw(master, first, second, gradient, decay):
    first_new = beta_one * first + (1.0 - beta_one) * gradient
    second_new = beta_two * second + (1.0 - beta_two) * gradient * gradient
    correct_one = 1.0 - beta_one ** (STEP + 1)
    correct_two = 1.0 - beta_two ** (STEP + 1)
    direction = first_new / correct_one / (jnp.sqrt(second_new / correct_two) + adam_epsilon)
    master_new = master - learning_rate * (direction + decay * master)
    return (master_new, first_new, second_new)


def exchange_kernel(
    dims, packed_ref, shard_ref, gathered_ref, adam_ref,
    r1, sb, r2, zb, r3, hb, r4, shards, masters,
    s1, t1, s2, t2, s3, t3, s4, t4, s5, t5, s6, t6, s7, t7, s8, t8,
):
    nx, ny, nzl, nzh = dims
    outer, inner = lax.axis_index("outer"), lax.axis_index("inner")
    core, x, zl = lax.rem(outer, NC), lax.rem(outer // NC, nx), outer // (NC * nx)
    y, zh = inner // nzh, lax.rem(inner, nzh)

    def device(x=x, y=y, zl=zl, zh=zh, core=core):
        return ((zl * nx + x) * NC + core, y * nzh + zh)

    def send(src, dst, s, t, to):
        copy = pltpu.make_async_remote_copy(
            src_ref=src, dst_ref=dst, send_sem=s, recv_sem=t, device_id=to, device_id_type=MESH
        )
        copy.start()
        return copy

    sibling = device(core=1 - core)
    plane = [(dx, dy) for dx in range(nx) for dy in range(ny)]
    others = plane[1:]
    ahead = {o: (lax.rem(x + o[0], nx), lax.rem(y + o[1], ny)) for o in plane}
    behind = {o: (lax.rem(x + nx - o[0], nx), lax.rem(y + ny - o[1], ny)) for o in plane}
    up_lo = [lax.rem(zl + d, nzl) for d in range(nzl)]
    up_hi = [lax.rem(zh + d, nzh) for d in range(nzh)]

    barrier = pltpu.get_barrier_semaphore()
    peers = [sibling]
    peers += [device(x=ahead[o][0], y=ahead[o][1]) for o in others]
    peers += [device(zl=z) for z in up_lo[1:]]
    peers += [device(zh=z) for z in up_hi[1:]]
    for peer in peers:
        pl.semaphore_signal(barrier, inc=1, device_id=peer, device_id_type=MESH)
    pl.semaphore_wait(barrier, len(peers))

    first = [
        send(packed_ref.at[1 - core, ahead[dx, 0][0]], r1.at[dx], s1.at[dx], t1.at[dx], sibling)
        for dx in range(nx)
    ]
    swaps = [
        send(shard_ref, shards.at[zh], s8.at[d], t8.at[d], device(zh=up_hi[d]))
        for d in range(1, nzh)
    ]
    shards[zh] = shard_ref[...]

    second = []
    for dx in range(nx):
        xs = ahead[dx, 0][0]
        first[dx].wait_recv()
        sb[xs] = (packed_ref[core, xs].astype(F32) + r1[dx].astype(F32)).astype(BF16)
        for dy in range(ny):
            o = dx, dy
            if o == (0, 0):
                continue
            ys = ahead[o][1]
            slot = dx * ny + dy - 1
            second.append(send(sb.at[xs, ys], r2.at[slot], s2.at[slot], t2.at[slot], device(x=xs, y=ys)))

    for c in swaps:
        c.wait_recv()
    for a in range(3):
        for h in range(nzh):
            for p in range(4):
                masters[a, p * nzh + h : p * nzh + h + 1, :] = shards[h, 4 * a + p : 4 * a + p + 1, :]

    total = sb[x, y].astype(F32)
    for slot in range(len(others)):
        second[slot].wait_recv()
        total = total + r2[slot].astype(F32)
    zb[...] = total.astype(BF16)

    third = [
        send(zb.at[up_lo[d]], r3.at[d], s3.at[d], t3.at[d], device(zl=up_lo[d]))
        for d in range(1, nzl)
    ]
    total = zb[zl].astype(F32)
    for c, d in zip(third, range(1, nzl)):
        c.wait_recv()
        total = total + r3[d].astype(F32)
    hb[...] = total.astype(BF16)

    fourth = [
        send(hb, r4.at[zh], s4.at[d], t4.at[d], device(zh=up_hi[d])) for d in range(1, nzh)
    ]
    r4[zh] = hb[...]
    for c in fourth:
        c.wait_recv()
    gradient = r4[0].astype(F32)
    for h in range(1, nzh):
        gradient = gradient + r4[h].astype(F32)

    rows = 4 * nzh
    is_gain = jnp.logical_and(iota((rows, LANES), 0) >= 3 * nzh, iota((rows, LANES), 1) >= ROPE)
    decay = jnp.where(is_gain, 0.0, 0.1)
    new = adamw(masters[0], masters[1], masters[2], gradient, decay)
    for a in range(3):
        adam_ref[a] = new[a]

    own = gathered_ref.at[core, x, y]
    gathered_ref[core, x, y, zl] = new[0].astype(BF16)
    fifth = [
        send(own.at[zl], own.at[zl], s5.at[d], t5.at[d], device(zl=up_lo[d]))
        for d in range(1, nzl)
    ]
    for c in fifth:
        c.wait_recv()
    sixth = [
        send(own, own, s6.at[i], t6.at[i], device(x=ahead[o][0], y=ahead[o][1]))
        for i, o in enumerate(others)
    ]
    seventh = [send(own, own, s7.at[len(others)], t7.at[len(others)], sibling)]
    for i, o in enumerate(others):
        sixth[i].wait_recv()
        part = gathered_ref.at[core, behind[o][0], behind[o][1]]
        seventh.append(send(part, part, s7.at[i], t7.at[i], sibling))
    for c in seventh:
        c.wait_recv()
    for c in first + swaps + second + third + fourth + fifth + sixth + seventh:
        c.wait_send()


def unpack_kernel(
    nzh, gathered_ref, adam_ref, weight_ref, gain_ref, wm_ref, wf_ref, ws_ref, gm_ref, gf_ref, gs_ref, wide, gains
):
    zh = lax.rem(lax.axis_index("inner"), nzh)
    for a, (w, g) in enumerate(((wm_ref, gm_ref), (wf_ref, gf_ref), (ws_ref, gs_ref))):
        for p in range(4):
            row = adam_ref[a, pl.ds(p * nzh + zh, 1), :]
            w[2 * p : 2 * p + 1, :] = row[:, :ROPE]
            if p < 3:
                w[2 * p + 1 : 2 * p + 2, :] = row[:, ROPE:]
            else:
                g[...] = row[:, ROPE : ROPE + OWN]

    upper = iota((16, 8, LANES), 1) < 4
    lane = iota((LANES, LANES), 1)
    for k in range(gathered_ref.shape[3]):
        even, odd = [], []
        for q in range(16):
            x, core, y = q // 4, (q // 2) % 2, 2 * (q % 2)
            even.append(gathered_ref[core, x, y, k].astype(F32).reshape(1, 16, LANES))
            odd.append(gathered_ref[core, x, y + 1, k].astype(F32).reshape(1, 16, LANES))
        even, odd = jnp.concatenate(even, axis=0), jnp.concatenate(odd, axis=0)
        tiles = []
        for i in range(2):
            e, o = even[:, 8 * i : 8 * i + 8], odd[:, 8 * i : 8 * i + 8]
            tiles.append(jnp.where(upper, e, pltpu.roll(o, 4, axis=1)))
            tiles.append(jnp.where(upper, pltpu.roll(e, 4, axis=1), o))
        tiles = [t.reshape(LANES, LANES) for t in tiles]
        for r in range(OWN):
            tile = tiles[r // 2]
            if r % 2:
                tile = pltpu.roll(tile, ROPE, axis=1)
            gain = jnp.where(lane == ROPE + r, tiles[3], 0.0)
            wide[k % 2, pl.ds(r, LANES, stride=OWN), :] = jnp.where(lane < ROPE, tile, gain)
        for i in range(OWN):
            at = OWN * k + i
            block = wide[k % 2, i * LANES : (i + 1) * LANES, :].T
            weight_ref[:, at * LANES : (at + 1) * LANES] = block[:ROPE].astype(BF16)
            gains[at : at + 1, :] = jnp.sum(block[ROPE : ROPE + 8], axis=0, keepdims=True)
    gain_ref[...] = gains[...].astype(BF16)


def vmem():
    return pl.BlockSpec(memory_space=pltpu.VMEM)


def shapes(*items):
    return [jax.ShapeDtypeStruct(s, t) for s, t in items]


def local_gradients(hidden, segment_ids, key_t, weight_t, gain, states):
    tokens, width = hidden.shape
    return pl.pallas_call(
        grads_kernel,
        out_shape=shapes(((NC, NX, NY, NZL, 16, LANES), BF16), ((16, LANES), F32)),
        in_specs=[vmem()] * 12,
        out_specs=[vmem()] * 2,
        scratch_shapes=[
            pltpu.VMEM((2 * LANES, LANES), F32),
            pltpu.VMEM((2, BLOCK, LANES), F32),
            pltpu.VMEM((8, 2 * LANES), jnp.int32),
            pltpu.VMEM((width // LANES, LANES), F32),
        ],
        compiler_params=pltpu.CompilerParams(vmem_limit_bytes=40 * 1024 * 1024),
    )(hidden, segment_ids, key_t, weight_t, gain, jnp.asarray(rotary_table()), *states)


def exchange(dims, packed, shard):
    nx, ny, nzl, nzh = dims
    rows = 4 * nzh
    tile = (rows, LANES)
    dma = pltpu.SemaphoreType.DMA
    planes = nx * ny
    counts = [nx, planes, nzl, nzh, nzl, planes, planes, nzh]
    return pl.pallas_call(
        functools.partial(exchange_kernel, dims),
        out_shape=shapes(((NC, nx, ny, nzl, *tile), BF16), ((3, *tile), F32)),
        in_specs=[vmem()] * 2,
        out_specs=[vmem()] * 2,
        scratch_shapes=[
            pltpu.VMEM((nx, ny, nzl, *tile), BF16),
            pltpu.VMEM((nx, ny, nzl, *tile), BF16),
            pltpu.VMEM((planes - 1, nzl, *tile), BF16),
            pltpu.VMEM((nzl, *tile), BF16),
            pltpu.VMEM((nzl, *tile), BF16),
            pltpu.VMEM(tile, BF16),
            pltpu.VMEM((nzh, *tile), BF16),
            pltpu.VMEM((nzh, 16, LANES), F32),
            pltpu.VMEM((3, *tile), F32),
        ]
        + [dma((n,)) for n in counts for _ in range(2)],
        compiler_params=pltpu.CompilerParams(
            collective_id=0, has_side_effects=True, vmem_limit_bytes=40 * 1024 * 1024
        ),
    )(packed, shard)


def unpack(gathered, adam, width):
    own = [((OWN, ROPE), F32)] * 3 + [((1, OWN), F32)] * 3
    return pl.pallas_call(
        functools.partial(unpack_kernel, NZH),
        out_shape=shapes(((ROPE, width), BF16), ((width // LANES, LANES), BF16), *own),
        in_specs=[vmem()] * 2,
        out_specs=[vmem()] * 8,
        scratch_shapes=[
            pltpu.VMEM((2, BLOCK, LANES), F32),
            pltpu.VMEM((width // LANES, LANES), F32),
        ],
        compiler_params=pltpu.CompilerParams(vmem_limit_bytes=40 * 1024 * 1024),
    )(gathered, adam)


def shards(
    hidden, segment_ids, key_grad, weight_bf16, gain_bf16,
    weight_master, weight_first, weight_second, gain_master, gain_first, gain_second,
):
    width = hidden.shape[1]
    states = [weight_master, weight_first, weight_second]
    states += [g.reshape(1, OWN) for g in (gain_master, gain_first, gain_second)]
    packed, shard = local_gradients(
        hidden, segment_ids, key_grad.T, weight_bf16.T, gain_bf16.reshape(width // LANES, LANES), states
    )
    gathered, adam = exchange((NX, NY, NZL, NZH), packed, shard)
    weight_t, gain, wm, wf, ws, gm, gf, gs = unpack(gathered, adam, width)
    return (
        wm, wf, ws, gm.reshape(OWN), gf.reshape(OWN), gs.reshape(OWN), weight_t.T, gain.reshape(width)
    )


def solution(mesh):
    both = P(("outer", "inner"), None)
    one = P(("outer", "inner"))
    return jax.shard_map(
        shards,
        mesh=mesh,
        in_specs=(both, both, both, P(), P(), both, both, both, one, one, one),
        out_specs=(both, both, both, one, one, one, P(), P()),
        check_vma=False,
    )
```

```python
import jax
import jax.numpy as jnp
import numpy as np
from jax import lax
from jax.experimental import pallas as pl
from jax.experimental.pallas import tpu as pltpu
from jax.sharding import PartitionSpec as P

STEP = 20
beta_one = 0.9
beta_two = 0.95
learning_rate = 0.00022
adam_epsilon = 1e-08
norm_epsilon = 1e-06

MESH = pl.DeviceIdType.MESH
F32 = jnp.float32
BF16 = jnp.bfloat16
ROPE = 64
HALF = ROPE // 2
OWN = 7
LANES = 128
BLOCK = OWN * LANES

NC, NX, NY, NZL, NZH = 2, 4, 4, 8, 4
NEAR = 4
FAR = NZL * NZH // NEAR
SPAN = NZL // NEAR
ROWS = 48


def rotary_table():
    frequency = 10000.0 ** (-np.arange(HALF) / HALF)
    angles = frequency[:, None] * np.arange(LANES)[None, :]
    return np.concatenate([np.cos(angles), np.sin(angles)]).astype(np.float32)


def iota(shape, axis):
    return lax.broadcasted_iota(jnp.int32, shape, axis)


def look_up(table, index):
    rows = [
        jnp.take_along_axis(table[8 * i : 8 * i + 8], index, axis=1)
        for i in range(table.shape[0] // 8)
    ]
    return jnp.concatenate(rows, axis=0)


def pack_shard(states):
    weight_ref, gain_ref = states
    gains = jnp.concatenate([gain_ref[...], jnp.zeros((1, ROPE - OWN), F32)], axis=1)
    rows = []
    for p in range(4):
        right = weight_ref[2 * p + 1 : 2 * p + 2, :] if p < 3 else gains
        rows.append(jnp.concatenate([weight_ref[2 * p : 2 * p + 1, :], right], axis=1))
    return rows


def latent_pair(seg_ref, key_ref, table_ref, segs, inverse_rms, tokens):
    padded = 2 * LANES
    segs[...] = jnp.full((8, padded), -1, jnp.int32)
    segs[:, :tokens] = jnp.broadcast_to(seg_ref[...], (8, tokens))
    ids = segs[...]
    lane = iota((8, padded), 1)
    begins = jnp.logical_or(ids != pltpu.roll(ids, 1, axis=1), lane == 0)
    start = jnp.where(begins, lane, 0)
    shift = 1
    while shift < padded:
        before = pltpu.roll(start, shift, axis=1)
        start = jnp.maximum(start, jnp.where(lane >= shift, before, 0))
        shift *= 2
    place = jnp.clip(lane - start, 0, LANES - 1)
    halves = [
        look_up(table_ref[...], place[:, i * LANES : (i + 1) * LANES]) for i in range(2)
    ]
    table = jnp.concatenate(halves, axis=1)[:, :tokens]
    cosine, sine = table[:HALF], table[HALF:]
    key = key_ref[...].astype(F32)
    a, b = key[:HALF], key[HALF:]
    latent = jnp.concatenate([a * cosine + b * sine, b * cosine - a * sine], axis=0)
    latent = latent.astype(BF16).astype(F32) * inverse_rms()
    high = latent.astype(BF16)
    low = (latent - high.astype(F32)).astype(BF16)
    return jnp.concatenate([high, low], axis=0)


def gradient_block(both, hidden, weight, gain_rows, wide):
    row8 = iota((8, LANES), 0)
    lane8 = iota((8, LANES), 1)
    left = iota((LANES, LANES), 1) < ROPE
    upper = iota((16, 8, LANES), 1) < 4
    product = jnp.dot(both, hidden, preferred_element_type=F32)
    product = product[:ROPE] + product[ROPE:]
    for i in range(OWN):
        part = product[:, i * LANES : (i + 1) * LANES]
        w = weight[:, i * LANES : (i + 1) * LANES].astype(F32)
        gain_grad = jnp.sum(w * part, axis=0, keepdims=True)
        chosen = row8 == lax.rem(lane8 + i * LANES, OWN)
        block = jnp.concatenate(
            [
                part * gain_rows(i),
                jnp.where(chosen, gain_grad, 0.0),
                jnp.zeros((LANES - ROPE - 8, LANES), F32),
            ],
            axis=0,
        )
        wide[i * LANES : (i + 1) * LANES, :] = block.T
    rows = [wide[pl.ds(r, LANES, stride=OWN), :] for r in range(OWN)]
    total = rows[0]
    for r in range(1, OWN):
        total = total + rows[r]
    tiles = [
        jnp.where(left, rows[2 * p], pltpu.roll(rows[2 * p + 1], ROPE, axis=1))
        for p in range(3)
    ]
    tiles.append(jnp.where(left, rows[6], total))
    tiles = [t.reshape(16, 8, LANES) for t in tiles]
    even, odd = [], []
    for one, two in ((tiles[0], tiles[1]), (tiles[2], tiles[3])):
        even.append(jnp.where(upper, one, pltpu.roll(two, 4, axis=1)))
        odd.append(jnp.where(upper, pltpu.roll(one, 4, axis=1), two))
    even = jnp.concatenate(even, axis=1).astype(BF16)
    odd = jnp.concatenate(odd, axis=1).astype(BF16)
    return even, odd


def adamw(master, first, second, gradient, decay):
    first_new = beta_one * first + (1.0 - beta_one) * gradient
    second_new = beta_two * second + (1.0 - beta_two) * gradient * gradient
    correct_one = 1.0 - beta_one ** (STEP + 1)
    correct_two = 1.0 - beta_two ** (STEP + 1)
    direction = first_new / correct_one / (jnp.sqrt(second_new / correct_two) + adam_epsilon)
    master_new = master - learning_rate * (direction + decay * master)
    return (master_new, first_new, second_new)


def step_kernel(
    hidden_hbm, seg_hbm, key_hbm, weight_hbm, gain_hbm, table_hbm,
    wm_hbm, wf_hbm, ws_hbm, gm_hbm, gf_hbm, gs_hbm,
    gathered_ref, adam_ref,
    hidden_ref, seg_ref, key_ref, weight_ref, gain_ref, table_ref,
    wm_ref, wf_ref, ws_ref, gm_ref, gf_ref, gs_ref,
    squares, wide, segs, gains, packed_ref, shard_ref,
    r1, sb, r2, zb, r3, hb, r4, shards, masters, in_sem, row_sem,
    s1, t1, s2, t2, s3, t3, s4, t4, s5, t5, s6, t6, s7, t7, s8, t8,
):
    tokens, width = hidden_ref.shape
    parts = tokens // ROWS
    outer, inner = lax.axis_index("outer"), lax.axis_index("inner")
    core, x = lax.rem(outer, NC), lax.rem(outer // NC, NX)
    y, z = inner // NZH, lax.rem(inner, NZH) * NZL + outer // (NC * NX)
    near, far = lax.rem(z, NEAR), z // NEAR

    def device(x=x, y=y, near=near, far=far, core=core):
        z = far * NEAR + near
        return ((lax.rem(z, NZL) * NX + x) * NC + core, y * NZH + z // NZL)

    loads = [
        pltpu.make_async_copy(src, dst, in_sem.at[i])
        for i, (src, dst) in enumerate(
            (
                (seg_hbm, seg_ref), (key_hbm, key_ref), (table_hbm, table_ref),
                (gain_hbm, gain_ref), (weight_hbm, weight_ref),
                (wm_hbm, wm_ref), (wf_hbm, wf_ref), (ws_hbm, ws_ref),
                (gm_hbm, gm_ref), (gf_hbm, gf_ref), (gs_hbm, gs_ref),
            )
        )
    ]

    def part_of_hidden(i):
        rows = pl.ds(pl.multiple_of(i * ROWS, 16), ROWS)
        return pltpu.make_async_copy(hidden_hbm.at[rows], hidden_ref.at[rows], row_sem.at[i])

    for load in loads[:4]:
        load.start()
    for i in range(parts):
        part_of_hidden(i).start()
    for load in loads[4:]:
        load.start()

    sibling = device(core=1 - core)
    plane = [(dx, dy) for dx in range(NX) for dy in range(NY)]
    others = plane[1:]
    ahead = {o: (lax.rem(x + o[0], NX), lax.rem(y + o[1], NY)) for o in plane}
    behind = {o: (lax.rem(x + NX - o[0], NX), lax.rem(y + NY - o[1], NY)) for o in plane}
    up_near = [lax.rem(near + d, NEAR) for d in range(NEAR)]
    up_far = [lax.rem(far + d, FAR) for d in range(FAR)]
    far_first = sorted(range(1, FAR), key=lambda d: -min(d, FAR - d))

    barrier = pltpu.get_barrier_semaphore()
    peers = [device(far=up_far[d]) for d in far_first]
    peers += [device(near=n) for n in up_near[1:]]
    peers += [device(x=ahead[o][0], y=ahead[o][1]) for o in others]
    peers += [sibling]
    for peer in peers:
        pl.semaphore_signal(barrier, inc=1, device_id=peer, device_id_type=MESH)

    def send(src, dst, s, t, to):
        copy = pltpu.make_async_remote_copy(
            src_ref=src, dst_ref=dst, send_sem=s, recv_sem=t, device_id=to, device_id_type=MESH
        )
        copy.start()
        return copy

    squares[tokens:, :] = jnp.zeros((2 * LANES - tokens, LANES), F32)

    def square(i, carry):
        part_of_hidden(i).wait()
        rows = pl.ds(pl.multiple_of(i * ROWS, 16), ROWS)
        total = jnp.zeros((ROWS, LANES), F32)
        for j in range(width // LANES):
            h = hidden_ref[rows, j * LANES : (j + 1) * LANES].astype(F32)
            total = total + h * h
        squares[rows, :] = total
        return carry

    def inverse_rms():
        lax.fori_loop(0, parts, square, 0)
        mean = jnp.sum(squares[...].T, axis=0, keepdims=True) * (1.0 / width)
        return lax.rsqrt(mean + norm_epsilon)[:, :tokens]

    for load in loads[:3]:
        load.wait()
    both = latent_pair(seg_ref, key_ref, table_ref, segs, inverse_rms, tokens)
    for load in loads[3:5]:
        load.wait()
    gains[...] = gain_ref[...].astype(F32)

    def block(k, carry):
        columns = pl.ds(pl.multiple_of(k * BLOCK, LANES), BLOCK)
        even, odd = gradient_block(
            both, hidden_ref[:, columns], weight_ref[:, columns],
            lambda i: gains[pl.ds(OWN * k + i, 1), :], wide,
        )
        n, h = lax.rem(k, NEAR), k // NEAR
        for q in range(16):
            xq, cq, yq = q // 4, (q // 2) % 2, 2 * (q % 2)
            packed_ref[cq, xq, yq, n, h] = even[q]
            packed_ref[cq, xq, yq + 1, n, h] = odd[q]
        return carry

    lax.fori_loop(0, width // BLOCK, block, 0)

    for load in loads[5:]:
        load.wait()
    for a, states in enumerate(((wm_ref, gm_ref), (wf_ref, gf_ref), (ws_ref, gs_ref))):
        for p, row in enumerate(pack_shard(states)):
            shard_ref[4 * a + p : 4 * a + p + 1, :] = row
    shard_ref[12:16, :] = jnp.ones((4, LANES), F32)

    pl.semaphore_wait(barrier, len(peers))

    first = [
        send(packed_ref.at[1 - core, ahead[dx, 0][0]], r1.at[dx], s1.at[dx], t1.at[dx], sibling)
        for dx in range(NX)
    ]
    swaps = [
        send(shard_ref, shards.at[far], s8.at[d], t8.at[d], device(far=up_far[d]))
        for d in far_first
    ]
    shards[far] = shard_ref[...]

    second = []
    for dx in range(NX):
        xs = ahead[dx, 0][0]
        first[dx].wait_recv()
        sb[xs] = (packed_ref[core, xs].astype(F32) + r1[dx].astype(F32)).astype(BF16)
        for dy in range(NY):
            o = dx, dy
            if o == (0, 0):
                continue
            ys = ahead[o][1]
            slot = dx * NY + dy - 1
            second.append(send(sb.at[xs, ys], r2.at[slot], s2.at[slot], t2.at[slot], device(x=xs, y=ys)))

    total = sb[x, y].astype(F32)
    for slot in range(len(others)):
        second[slot].wait_recv()
        total = total + r2[slot].astype(F32)
    zb[...] = total.astype(BF16)

    third = [
        send(zb.at[up_near[d]], r3.at[d], s3.at[d], t3.at[d], device(near=up_near[d]))
        for d in range(1, NEAR)
    ]

    for c in swaps:
        c.wait_recv()
    for a in range(3):
        for f in range(FAR):
            for p in range(4):
                row = p * NZH + f // SPAN
                masters[a, f % SPAN, row : row + 1, :] = shards[f, 4 * a + p : 4 * a + p + 1, :]

    total = zb[near].astype(F32)
    for c, d in zip(third, range(1, NEAR)):
        c.wait_recv()
        total = total + r3[d].astype(F32)
    hb[...] = total.astype(BF16)

    fourth = [
        send(hb, r4.at[far], s4.at[d], t4.at[d], device(far=up_far[d])) for d in far_first
    ]
    r4[far] = hb[...]
    for c in fourth:
        c.wait_recv()
    gradient = r4[0].astype(F32)
    for f in range(1, FAR):
        gradient = gradient + r4[f].astype(F32)

    tile = gradient.shape
    is_gain = jnp.logical_and(iota(tile, 1) >= 3 * NZH, iota(tile, 2) >= ROPE)
    decay = jnp.where(is_gain, 0.0, 0.1)
    new = adamw(masters[0], masters[1], masters[2], gradient, decay)
    for a in range(3):
        adam_ref[a] = new[a]

    own = gathered_ref.at[core, x, y]
    gathered_ref[core, x, y, near] = new[0].astype(BF16)
    fifth = [
        send(own.at[near], own.at[near], s5.at[d], t5.at[d], device(near=up_near[d]))
        for d in range(1, NEAR)
    ]
    for c in fifth:
        c.wait_recv()
    sixth = [
        send(own, own, s6.at[i], t6.at[i], device(x=ahead[o][0], y=ahead[o][1]))
        for i, o in enumerate(others)
    ]
    seventh = [send(own, own, s7.at[len(others)], t7.at[len(others)], sibling)]
    for i, o in enumerate(others):
        sixth[i].wait_recv()
        part = gathered_ref.at[core, behind[o][0], behind[o][1]]
        seventh.append(send(part, part, s7.at[i], t7.at[i], sibling))
    for c in seventh:
        c.wait_recv()
    for c in first + swaps + second + third + fourth + fifth + sixth + seventh:
        c.wait_send()


def unpack_kernel(
    gathered_hbm, adam_hbm, weight_ref, gain_ref, wm_ref, wf_ref, ws_ref, gm_ref, gf_ref, gs_ref,
    gathered_ref, adam_ref, wide, gains, in_sem,
):
    loads = [
        pltpu.make_async_copy(
            gathered_hbm.at[:, :, :, n], gathered_ref.at[:, :, :, n], in_sem.at[n]
        )
        for n in range(NEAR)
    ]
    loads.append(pltpu.make_async_copy(adam_hbm, adam_ref, in_sem.at[NEAR]))
    for load in loads:
        load.start()
    upper = iota((16, 8, LANES), 1) < 4
    lane = iota((LANES, LANES), 1)
    for turn in range(NZL):
        n, h = turn // SPAN, turn % SPAN
        k = h * NEAR + n
        if h == 0:
            loads[n].wait()
        even, odd = [], []
        for q in range(16):
            x, core, y = q // 4, (q // 2) % 2, 2 * (q % 2)
            even.append(gathered_ref[core, x, y, n, h].astype(F32).reshape(1, 16, LANES))
            odd.append(gathered_ref[core, x, y + 1, n, h].astype(F32).reshape(1, 16, LANES))
        even, odd = jnp.concatenate(even, axis=0), jnp.concatenate(odd, axis=0)
        tiles = []
        for i in range(2):
            e, o = even[:, 8 * i : 8 * i + 8], odd[:, 8 * i : 8 * i + 8]
            tiles.append(jnp.where(upper, e, pltpu.roll(o, 4, axis=1)))
            tiles.append(jnp.where(upper, pltpu.roll(e, 4, axis=1), o))
        tiles = [t.reshape(LANES, LANES) for t in tiles]
        for r in range(OWN):
            tile = tiles[r // 2]
            if r % 2:
                tile = pltpu.roll(tile, ROPE, axis=1)
            gain = jnp.where(lane == ROPE + r, tiles[3], 0.0)
            wide[turn % 2, pl.ds(r, LANES, stride=OWN), :] = jnp.where(lane < ROPE, tile, gain)
        for i in range(OWN):
            at = OWN * k + i
            block = wide[turn % 2, i * LANES : (i + 1) * LANES, :].T
            weight_ref[:, at * LANES : (at + 1) * LANES] = block[:ROPE].astype(BF16)
            gains[at : at + 1, :] = jnp.sum(block[ROPE : ROPE + 8], axis=0, keepdims=True)
    gain_ref[...] = gains[...].astype(BF16)
    loads[NEAR].wait()
    zh = lax.rem(lax.axis_index("inner"), NZH)
    zl = lax.axis_index("outer") // (NC * NX)
    for a, (w, g) in enumerate(((wm_ref, gm_ref), (wf_ref, gf_ref), (ws_ref, gs_ref))):
        for p in range(4):
            row = adam_ref[a, zl // NEAR, pl.ds(p * NZH + zh, 1), :]
            w[2 * p : 2 * p + 1, :] = row[:, :ROPE]
            if p < 3:
                w[2 * p + 1 : 2 * p + 2, :] = row[:, ROPE:]
            else:
                g[...] = row[:, ROPE : ROPE + OWN]


def vmem():
    return pl.BlockSpec(memory_space=pltpu.VMEM)


def shapes(*items):
    return [jax.ShapeDtypeStruct(s, t) for s, t in items]


def step(operands):
    hidden = operands[0]
    tokens, width = hidden.shape
    dma = pltpu.SemaphoreType.DMA
    piece = (SPAN, 16, LANES)
    others = NX * NY - 1
    chunk = (NEAR, *piece)
    counts = [NX, others, NEAR, FAR, NEAR, others, others + 1, FAR]
    return pl.pallas_call(
        step_kernel,
        out_shape=shapes(((NC, NX, NY, *chunk), BF16), ((3, *piece), F32)),
        in_specs=[pl.BlockSpec(memory_space=pltpu.HBM)] * len(operands),
        out_specs=[vmem()] * 2,
        scratch_shapes=[pltpu.VMEM(o.shape, o.dtype) for o in operands]
        + [
            pltpu.VMEM((2 * LANES, LANES), F32),
            pltpu.VMEM((BLOCK, LANES), F32),
            pltpu.VMEM((8, 2 * LANES), jnp.int32),
            pltpu.VMEM((width // LANES, LANES), F32),
            pltpu.VMEM((NC, NX, NY, *chunk), BF16),
            pltpu.VMEM((16, LANES), F32),
            pltpu.VMEM((NX, NY, *chunk), BF16),
            pltpu.VMEM((NX, NY, *chunk), BF16),
            pltpu.VMEM((others, *chunk), BF16),
            pltpu.VMEM(chunk, BF16),
            pltpu.VMEM(chunk, BF16),
            pltpu.VMEM(piece, BF16),
            pltpu.VMEM((FAR, *piece), BF16),
            pltpu.VMEM((FAR, 16, LANES), F32),
            pltpu.VMEM((3, *piece), F32),
            dma((len(operands) - 1,)),
            dma((tokens // ROWS,)),
        ]
        + [dma((n,)) for n in counts for _ in range(2)],
        compiler_params=pltpu.CompilerParams(
            collective_id=0, has_side_effects=True, vmem_limit_bytes=56 * 1024 * 1024
        ),
    )(*operands)


def unpack(gathered, adam, width):
    own = [((OWN, ROPE), F32)] * 3 + [((1, OWN), F32)] * 3
    return pl.pallas_call(
        unpack_kernel,
        out_shape=shapes(((ROPE, width), BF16), ((width // LANES, LANES), BF16), *own),
        in_specs=[pl.BlockSpec(memory_space=pltpu.HBM)] * 2,
        out_specs=[vmem()] * 8,
        scratch_shapes=[
            pltpu.VMEM(gathered.shape, gathered.dtype),
            pltpu.VMEM(adam.shape, adam.dtype),
            pltpu.VMEM((2, BLOCK, LANES), F32),
            pltpu.VMEM((width // LANES, LANES), F32),
            pltpu.SemaphoreType.DMA((NEAR + 1,)),
        ],
        compiler_params=pltpu.CompilerParams(vmem_limit_bytes=56 * 1024 * 1024),
    )(gathered, adam)


def shards(
    hidden, segment_ids, key_grad, weight_bf16, gain_bf16,
    weight_master, weight_first, weight_second, gain_master, gain_first, gain_second,
):
    width = hidden.shape[1]
    states = [weight_master, weight_first, weight_second]
    states += [g.reshape(1, OWN) for g in (gain_master, gain_first, gain_second)]
    operands = [hidden, segment_ids, key_grad.T, weight_bf16.T, gain_bf16.reshape(width // LANES, LANES)]
    gathered, adam = step([*operands, jnp.asarray(rotary_table()), *states])
    weight_t, gain, wm, wf, ws, gm, gf, gs = unpack(gathered, adam, width)
    return (
        wm, wf, ws, gm.reshape(OWN), gf.reshape(OWN), gs.reshape(OWN), weight_t.T, gain.reshape(width)
    )


def solution(mesh):
    both = P(("outer", "inner"), None)
    one = P(("outer", "inner"))
    return jax.shard_map(
        shards,
        mesh=mesh,
        in_specs=(both, both, both, P(), P(), both, both, both, one, one, one),
        out_specs=(both, both, both, one, one, one, P(), P()),
        check_vma=False,
    )
```

```python
import jax
import jax.numpy as jnp
import numpy as np
from jax import lax
from jax.experimental import pallas as pl
from jax.experimental.pallas import tpu as pltpu
from jax.sharding import PartitionSpec as P

STEP = 20
beta_one = 0.9
beta_two = 0.95
learning_rate = 0.00022
adam_epsilon = 1e-08
norm_epsilon = 1e-06

MESH = pl.DeviceIdType.MESH
F32 = jnp.float32
BF16 = jnp.bfloat16
ROPE = 64
HALF = ROPE // 2
OWN = 7
LANES = 128
BLOCK = OWN * LANES

NC, NX, NY, NZL, NZH = 2, 4, 4, 8, 4
NEAR = 4
FAR = NZL * NZH // NEAR
SPAN = NZL // NEAR
ROWS = 48


def rotary_table():
    frequency = 10000.0 ** (-np.arange(HALF) / HALF)
    angles = frequency[:, None] * np.arange(LANES)[None, :]
    return np.concatenate([np.cos(angles), np.sin(angles)]).astype(np.float32)


def iota(shape, axis):
    return lax.broadcasted_iota(jnp.int32, shape, axis)


def look_up(table, index):
    rows = [
        jnp.take_along_axis(table[8 * i : 8 * i + 8], index, axis=1)
        for i in range(table.shape[0] // 8)
    ]
    return jnp.concatenate(rows, axis=0)


def pack_shard(states):
    weight_ref, gain_ref = states
    gains = jnp.concatenate([gain_ref[...], jnp.zeros((1, ROPE - OWN), F32)], axis=1)
    rows = []
    for p in range(4):
        right = weight_ref[2 * p + 1 : 2 * p + 2, :] if p < 3 else gains
        rows.append(jnp.concatenate([weight_ref[2 * p : 2 * p + 1, :], right], axis=1))
    return rows


def latent_pair(seg_ref, key_ref, table_ref, segs, inverse_rms, tokens):
    padded = 2 * LANES
    segs[...] = jnp.full((8, padded), -1, jnp.int32)
    segs[:, :tokens] = jnp.broadcast_to(seg_ref[...], (8, tokens))
    ids = segs[...]
    lane = iota((8, padded), 1)
    begins = jnp.logical_or(ids != pltpu.roll(ids, 1, axis=1), lane == 0)
    start = jnp.where(begins, lane, 0)
    shift = 1
    while shift < padded:
        before = pltpu.roll(start, shift, axis=1)
        start = jnp.maximum(start, jnp.where(lane >= shift, before, 0))
        shift *= 2
    place = jnp.clip(lane - start, 0, LANES - 1)
    halves = [
        look_up(table_ref[...], place[:, i * LANES : (i + 1) * LANES]) for i in range(2)
    ]
    table = jnp.concatenate(halves, axis=1)[:, :tokens]
    cosine, sine = table[:HALF], table[HALF:]
    key = key_ref[...].astype(F32)
    a, b = key[:HALF], key[HALF:]
    latent = jnp.concatenate([a * cosine + b * sine, b * cosine - a * sine], axis=0)
    latent = latent.astype(BF16).astype(F32) * inverse_rms()
    high = latent.astype(BF16)
    low = (latent - high.astype(F32)).astype(BF16)
    return jnp.concatenate([high, low], axis=0)


def gradient_block(both, hidden, weight, gain_rows, wide):
    row8 = iota((8, LANES), 0)
    lane8 = iota((8, LANES), 1)
    left = iota((LANES, LANES), 1) < ROPE
    upper = iota((16, 8, LANES), 1) < 4
    product = jnp.dot(both, hidden, preferred_element_type=F32)
    product = product[:ROPE] + product[ROPE:]
    for i in range(OWN):
        part = product[:, i * LANES : (i + 1) * LANES]
        w = weight[:, i * LANES : (i + 1) * LANES].astype(F32)
        gain_grad = jnp.sum(w * part, axis=0, keepdims=True)
        chosen = row8 == lax.rem(lane8 + i * LANES, OWN)
        block = jnp.concatenate(
            [
                part * gain_rows(i),
                jnp.where(chosen, gain_grad, 0.0),
                jnp.zeros((LANES - ROPE - 8, LANES), F32),
            ],
            axis=0,
        )
        wide[i * LANES : (i + 1) * LANES, :] = block.T
    rows = [wide[pl.ds(r, LANES, stride=OWN), :] for r in range(OWN)]
    total = rows[0]
    for r in range(1, OWN):
        total = total + rows[r]
    tiles = [
        jnp.where(left, rows[2 * p], pltpu.roll(rows[2 * p + 1], ROPE, axis=1))
        for p in range(3)
    ]
    tiles.append(jnp.where(left, rows[6], total))
    tiles = [t.reshape(16, 8, LANES) for t in tiles]
    even, odd = [], []
    for one, two in ((tiles[0], tiles[1]), (tiles[2], tiles[3])):
        even.append(jnp.where(upper, one, pltpu.roll(two, 4, axis=1)))
        odd.append(jnp.where(upper, pltpu.roll(one, 4, axis=1), two))
    even = jnp.concatenate(even, axis=1).astype(BF16)
    odd = jnp.concatenate(odd, axis=1).astype(BF16)
    return even, odd


def adamw(master, first, second, gradient, decay):
    first_new = beta_one * first + (1.0 - beta_one) * gradient
    second_new = beta_two * second + (1.0 - beta_two) * gradient * gradient
    correct_one = 1.0 - beta_one ** (STEP + 1)
    correct_two = 1.0 - beta_two ** (STEP + 1)
    direction = first_new / correct_one / (jnp.sqrt(second_new / correct_two) + adam_epsilon)
    master_new = master - learning_rate * (direction + decay * master)
    return (master_new, first_new, second_new)


def step_kernel(
    hidden_hbm, seg_hbm, key_hbm, weight_hbm, gain_hbm, table_hbm,
    wm_hbm, wf_hbm, ws_hbm, gm_hbm, gf_hbm, gs_hbm,
    gathered_hbm, adam_ref,
    gathered_ref, hidden_ref, seg_ref, key_ref, weight_ref, gain_ref, table_ref,
    wm_ref, wf_ref, ws_ref, gm_ref, gf_ref, gs_ref,
    squares, wide, segs, gains, packed_ref, shard_ref,
    r1, sb, r2, zb, r3, hb, r4, mine, shards, masters, sums, in_sem, row_sem, met, out_sem,
    s1, t1, s2, t2, s3, t3, s4, t4, s5, t5, s6, t6, s7, t7, s8, t8,
):
    tokens, width = hidden_ref.shape
    parts = tokens // ROWS
    outer, inner = lax.axis_index("outer"), lax.axis_index("inner")
    core, x = lax.rem(outer, NC), lax.rem(outer // NC, NX)
    y, z = inner // NZH, lax.rem(inner, NZH) * NZL + outer // (NC * NX)
    near, far = lax.rem(z, NEAR), z // NEAR

    def device(x=x, y=y, near=near, far=far, core=core):
        z = far * NEAR + near
        return ((lax.rem(z, NZL) * NX + x) * NC + core, y * NZH + z // NZL)

    loads = [
        pltpu.make_async_copy(src, dst, in_sem.at[i])
        for i, (src, dst) in enumerate(
            (
                (seg_hbm, seg_ref), (key_hbm, key_ref), (table_hbm, table_ref),
                (gain_hbm, gain_ref), (weight_hbm, weight_ref),
                (wm_hbm, wm_ref), (wf_hbm, wf_ref), (ws_hbm, ws_ref),
                (gm_hbm, gm_ref), (gf_hbm, gf_ref), (gs_hbm, gs_ref),
            )
        )
    ]

    def part_of_hidden(i):
        rows = pl.ds(pl.multiple_of(i * ROWS, 16), ROWS)
        return pltpu.make_async_copy(hidden_hbm.at[rows], hidden_ref.at[rows], row_sem.at[i])

    for load in loads[:4]:
        load.start()
    for i in range(parts):
        part_of_hidden(i).start()
    for load in loads[4:]:
        load.start()

    sibling = device(core=1 - core)
    order_x = sorted(range(NX), key=lambda d: (d == 0, -min(d, NX - d)))
    order_y = sorted(range(NY), key=lambda d: -min(d, NY - d))
    plane = [(dx, dy) for dx in order_x for dy in order_y]
    others = [o for o in plane if o != (0, 0)]
    ahead = {o: (lax.rem(x + o[0], NX), lax.rem(y + o[1], NY)) for o in plane}
    behind = {o: (lax.rem(x + NX - o[0], NX), lax.rem(y + NY - o[1], NY)) for o in plane}
    up_near = [lax.rem(near + d, NEAR) for d in range(NEAR)]
    quarters = [up_near[(t + 1) % NEAR] for t in range(NEAR)]
    behind_near = [lax.rem(near + NEAR - d, NEAR) for d in range(NEAR)]
    up_far = [lax.rem(far + d, FAR) for d in range(FAR)]
    far_first = sorted(range(1, FAR), key=lambda d: -min(d, FAR - d))

    barrier = pltpu.get_barrier_semaphore()
    reach = [1 << i for i in range((FAR // 2).bit_length() - 1)]
    steps = [[device(far=up_far[d]), device(far=up_far[FAR - d])] for d in reach]
    peers = list(steps[0])
    peers += [device(near=n) for n in up_near[1:]]
    peers += [device(x=ahead[o][0], y=ahead[o][1]) for o in others]
    peers += [sibling]
    for peer in peers:
        pl.semaphore_signal(barrier, inc=1, device_id=peer, device_id_type=MESH)

    def send(src, dst, s, t, to):
        copy = pltpu.make_async_remote_copy(
            src_ref=src, dst_ref=dst, send_sem=s, recv_sem=t, device_id=to, device_id_type=MESH
        )
        copy.start()
        return copy

    squares[tokens:, :] = jnp.zeros((2 * LANES - tokens, LANES), F32)

    def square(i, carry):
        part_of_hidden(i).wait()
        rows = pl.ds(pl.multiple_of(i * ROWS, 16), ROWS)
        total = jnp.zeros((ROWS, LANES), F32)
        for j in range(width // LANES):
            h = hidden_ref[rows, j * LANES : (j + 1) * LANES].astype(F32)
            total = total + h * h
        squares[rows, :] = total
        return carry

    def inverse_rms():
        lax.fori_loop(0, parts, square, 0)
        mean = jnp.sum(squares[...].T, axis=0, keepdims=True) * (1.0 / width)
        return lax.rsqrt(mean + norm_epsilon)[:, :tokens]

    for load in loads[:3]:
        load.wait()
    both = latent_pair(seg_ref, key_ref, table_ref, segs, inverse_rms, tokens)
    for load in loads[3:5]:
        load.wait()
    gains[...] = gain_ref[...].astype(F32)

    pl.semaphore_wait(barrier, len(peers))
    for peer in steps[0]:
        pl.semaphore_signal(met.at[0], inc=1, device_id=peer, device_id_type=MESH)

    def gradients(t):
        n = quarters[t]
        for h in range(SPAN):
            k = h * NEAR + n
            columns = pl.ds(pl.multiple_of(k * BLOCK, LANES), BLOCK)
            even, odd = gradient_block(
                both, hidden_ref[:, columns], weight_ref[:, columns],
                lambda i: gains[pl.ds(OWN * k + i, 1), :], wide.at[h],
            )
            for q in range(16):
                xq, cq, yq = q // 4, (q // 2) % 2, 2 * (q % 2)
                packed_ref[t, cq, xq, yq, h] = even[q]
                packed_ref[t, cq, xq, yq + 1, h] = odd[q]

    def halves(t):
        return send(packed_ref.at[t, 1 - core], r1.at[t], s1.at[t], t1.at[t], sibling)

    def to_plane(t):
        first[t].wait_recv()
        sb[t] = (packed_ref[t, core].astype(F32) + r1[t].astype(F32)).astype(BF16)
        for i, o in enumerate(others):
            xs, ys = ahead[o]
            send(sb.at[t, xs, ys], r2.at[t, i], s2, t2.at[t], device(x=xs, y=ys))

    first = []
    for t in range(NEAR):
        gradients(t)
        first.append(halves(t))
        if t > 0:
            to_plane(t - 1)
        if t == NEAR - 1:
            for i in range(1, len(steps)):
                pl.semaphore_wait(met.at[i - 1], 2)
                for peer in steps[i]:
                    pl.semaphore_signal(met.at[i], inc=1, device_id=peer, device_id_type=MESH)

    for load in loads[5:]:
        load.wait()
    for a, states in enumerate(((wm_ref, gm_ref), (wf_ref, gf_ref), (ws_ref, gs_ref))):
        for p, row in enumerate(pack_shard(states)):
            shard_ref[4 * a + p : 4 * a + p + 1, :] = row
    shard = shard_ref[0:12, :]
    master = shard[0:4].astype(BF16).astype(F32)
    mine[...] = jnp.concatenate([master, shard[0:4] - master, shard[4:12]], axis=0).astype(BF16)

    to_plane(NEAR - 1)

    third = []
    for t in range(NEAR):
        pltpu.make_async_copy(r2.at[t], r2.at[t], t2.at[t]).wait()
        total = sb[t, x, y].astype(F32)
        for i in range(len(others)):
            total = total + r2[t, i].astype(F32)
        if t < NEAR - 1:
            zb[t] = total.astype(BF16)
            third.append(
                send(zb.at[t], r3.at[t], s3.at[t], t3.at[t], device(near=quarters[t]))
            )
        if t == 0:
            pl.semaphore_wait(met.at[len(steps) - 1], 2)
            swaps = [
                send(mine, shards.at[far], s8.at[d], t8.at[d], device(far=up_far[d]))
                for d in far_first
            ]
            shards[far] = mine[...]
    for t in range(NEAR - 1):
        third[t].wait_recv()
        total = total + r3[t].astype(F32)
    hb[...] = total.astype(BF16)

    fourth = [
        send(hb, r4.at[far], s4.at[d], t4.at[d], device(far=up_far[d])) for d in far_first
    ]
    r4[far] = hb[...]
    for c in first + third:
        c.wait_send()
    pltpu.make_async_copy(r2, r2, s2).wait()

    for c in swaps:
        c.wait_recv()
    for f in range(FAR):
        state = shards[f].astype(F32)
        state = [state[0:4] + state[4:8], state[8:12], state[12:16]]
        for a in range(3):
            for p in range(4):
                row = p * NZH + f // SPAN
                masters[a, f % SPAN, row : row + 1, :] = state[a][p : p + 1]

    for c in fourth:
        c.wait_recv()
    gradient = r4[0].astype(F32)
    for f in range(1, FAR):
        gradient = gradient + r4[f].astype(F32)

    tile = gradient.shape
    is_gain = jnp.logical_and(iota(tile, 1) >= 3 * NZH, iota(tile, 2) >= ROPE)
    decay = jnp.where(is_gain, 0.0, 0.1)
    new = adamw(masters[0], masters[1], masters[2], gradient, decay)

    own = gathered_ref.at[core, :, x, y]
    gathered_ref[core, near, x, y] = new[0].astype(BF16)
    fifth = [
        send(own.at[near], own.at[near], s5.at[d], t5.at[d], device(near=up_near[d]))
        for d in range(1, NEAR)
    ]

    sums[...] = gradient
    zh = z // NZL
    gradient = [sums[lax.rem(far, SPAN), pl.ds(p * NZH + zh, 1), :] for p in range(4)]
    is_gain = jnp.logical_and(iota((4, LANES), 0) == 3, iota((4, LANES), 1) >= ROPE)
    decay = jnp.where(is_gain, 0.0, 0.1)
    shard = shard_ref[0:12, :]
    new = adamw(shard[0:4], shard[4:8], shard[8:12], jnp.concatenate(gradient, axis=0), decay)
    for a in range(3):
        adam_ref[4 * a : 4 * a + 4, :] = new[a]
    for c in swaps + fourth:
        c.wait_send()

    for d in range(NEAR):
        if d > 0:
            fifth[d - 1].wait_recv()
        tile = own.at[behind_near[d]]
        for o in others:
            send(tile, tile, s6, t6.at[d], device(x=ahead[o][0], y=ahead[o][1]))
    for c in fifth:
        c.wait_send()

    out = []
    for d in range(NEAR):
        n = behind_near[d]
        pltpu.make_async_copy(r2.at[d], r2.at[d], t6.at[d]).wait()
        part = gathered_ref.at[core, n]
        send(part, part, s7, t7.at[d], sibling)
        out.append(pltpu.make_async_copy(part, gathered_hbm.at[core, n], out_sem.at[2 * d]))
        out[-1].start()
    for d in range(NEAR):
        n = behind_near[d]
        part = gathered_ref.at[1 - core, n]
        pltpu.make_async_copy(part, part, t7.at[d]).wait()
        out.append(pltpu.make_async_copy(part, gathered_hbm.at[1 - core, n], out_sem.at[2 * d + 1]))
        out[-1].start()
    pltpu.make_async_copy(r2, r2, s6).wait()
    half = gathered_ref.at[0]
    pltpu.make_async_copy(half, half, s7).wait()
    for c in out:
        c.wait()


def unpack_kernel(
    gathered_hbm, adam_hbm, weight_ref, gain_ref, wm_ref, wf_ref, ws_ref, gm_ref, gf_ref, gs_ref,
    gathered_ref, adam_ref, wide, gains, in_sem,
):
    loads = [
        pltpu.make_async_copy(
            gathered_hbm.at[:, n], gathered_ref.at[:, n], in_sem.at[n]
        )
        for n in range(NEAR)
    ]
    loads.append(pltpu.make_async_copy(adam_hbm, adam_ref, in_sem.at[NEAR]))
    for load in loads:
        load.start()
    upper = iota((16, 8, LANES), 1) < 4
    lane = iota((LANES, LANES), 1)
    for turn in range(NZL):
        n, h = turn // SPAN, turn % SPAN
        k = h * NEAR + n
        if h == 0:
            loads[n].wait()
        even, odd = [], []
        for q in range(16):
            x, core, y = q // 4, (q // 2) % 2, 2 * (q % 2)
            even.append(gathered_ref[core, n, x, y, h].astype(F32).reshape(1, 16, LANES))
            odd.append(gathered_ref[core, n, x, y + 1, h].astype(F32).reshape(1, 16, LANES))
        even, odd = jnp.concatenate(even, axis=0), jnp.concatenate(odd, axis=0)
        tiles = []
        for i in range(2):
            e, o = even[:, 8 * i : 8 * i + 8], odd[:, 8 * i : 8 * i + 8]
            tiles.append(jnp.where(upper, e, pltpu.roll(o, 4, axis=1)))
            tiles.append(jnp.where(upper, pltpu.roll(e, 4, axis=1), o))
        tiles = [t.reshape(LANES, LANES) for t in tiles]
        for r in range(OWN):
            tile = tiles[r // 2]
            if r % 2:
                tile = pltpu.roll(tile, ROPE, axis=1)
            gain = jnp.where(lane == ROPE + r, tiles[3], 0.0)
            wide[turn % 2, pl.ds(r, LANES, stride=OWN), :] = jnp.where(lane < ROPE, tile, gain)
        for i in range(OWN):
            at = OWN * k + i
            block = wide[turn % 2, i * LANES : (i + 1) * LANES, :].T
            weight_ref[:, at * LANES : (at + 1) * LANES] = block[:ROPE].astype(BF16)
            gains[at : at + 1, :] = jnp.sum(block[ROPE : ROPE + 8], axis=0, keepdims=True)
    gain_ref[...] = gains[...].astype(BF16)
    loads[NEAR].wait()
    for a, (w, g) in enumerate(((wm_ref, gm_ref), (wf_ref, gf_ref), (ws_ref, gs_ref))):
        for p in range(4):
            row = adam_ref[4 * a + p : 4 * a + p + 1, :]
            w[2 * p : 2 * p + 1, :] = row[:, :ROPE]
            if p < 3:
                w[2 * p + 1 : 2 * p + 2, :] = row[:, ROPE:]
            else:
                g[...] = row[:, ROPE : ROPE + OWN]


def vmem():
    return pl.BlockSpec(memory_space=pltpu.VMEM)


def shapes(*items):
    return [jax.ShapeDtypeStruct(s, t) for s, t in items]


def step(operands):
    hidden = operands[0]
    tokens, width = hidden.shape
    dma = pltpu.SemaphoreType.DMA
    piece = (SPAN, 16, LANES)
    others = NX * NY - 1
    chunk = (NEAR, *piece)
    counts = [NEAR, NEAR, 0, NEAR, NEAR, NEAR, FAR, FAR, NEAR, NEAR, 0, NEAR, 0, NEAR, FAR, FAR]
    return pl.pallas_call(
        step_kernel,
        out_shape=shapes(((NC, NEAR, NX, NY, *piece), BF16), ((16, LANES), F32)),
        in_specs=[pl.BlockSpec(memory_space=pltpu.HBM)] * len(operands),
        out_specs=[pl.BlockSpec(memory_space=pltpu.HBM), vmem()],
        scratch_shapes=[pltpu.VMEM((NC, NEAR, NX, NY, *piece), BF16)]
        + [pltpu.VMEM(o.shape, o.dtype) for o in operands]
        + [
            pltpu.VMEM((2 * LANES, LANES), F32),
            pltpu.VMEM((SPAN, BLOCK, LANES), F32),
            pltpu.VMEM((8, 2 * LANES), jnp.int32),
            pltpu.VMEM((width // LANES, LANES), F32),
            pltpu.VMEM((NEAR, NC, NX, NY, *piece), BF16),
            pltpu.VMEM((16, LANES), F32),
            pltpu.VMEM((NEAR, NX, NY, *piece), BF16),
            pltpu.VMEM((NEAR, NX, NY, *piece), BF16),
            pltpu.VMEM((NEAR, others, *piece), BF16),
            pltpu.VMEM(chunk, BF16),
            pltpu.VMEM(chunk, BF16),
            pltpu.VMEM(piece, BF16),
            pltpu.VMEM((FAR, *piece), BF16),
            pltpu.VMEM((16, LANES), BF16),
            pltpu.VMEM((FAR, 16, LANES), BF16),
            pltpu.VMEM((3, *piece), F32),
            pltpu.VMEM(piece, F32),
            dma((len(operands) - 1,)),
            dma((tokens // ROWS,)),
            pltpu.SemaphoreType.REGULAR((2,)),
            dma((2 * NEAR,)),
        ]
        + [dma((n,)) if n else dma for n in counts],
        compiler_params=pltpu.CompilerParams(
            collective_id=0, has_side_effects=True, vmem_limit_bytes=56 * 1024 * 1024
        ),
    )(*operands)


def unpack(gathered, adam, width):
    own = [((OWN, ROPE), F32)] * 3 + [((1, OWN), F32)] * 3
    return pl.pallas_call(
        unpack_kernel,
        out_shape=shapes(((ROPE, width), BF16), ((width // LANES, LANES), BF16), *own),
        in_specs=[pl.BlockSpec(memory_space=pltpu.HBM)] * 2,
        out_specs=[vmem()] * 8,
        scratch_shapes=[
            pltpu.VMEM(gathered.shape, gathered.dtype),
            pltpu.VMEM(adam.shape, adam.dtype),
            pltpu.VMEM((2, BLOCK, LANES), F32),
            pltpu.VMEM((width // LANES, LANES), F32),
            pltpu.SemaphoreType.DMA((NEAR + 1,)),
        ],
        compiler_params=pltpu.CompilerParams(vmem_limit_bytes=56 * 1024 * 1024),
    )(gathered, adam)


def shards(
    hidden, segment_ids, key_grad, weight_bf16, gain_bf16,
    weight_master, weight_first, weight_second, gain_master, gain_first, gain_second,
):
    width = hidden.shape[1]
    states = [weight_master, weight_first, weight_second]
    states += [g.reshape(1, OWN) for g in (gain_master, gain_first, gain_second)]
    operands = [hidden, segment_ids, key_grad.T, weight_bf16.T, gain_bf16.reshape(width // LANES, LANES)]
    gathered, adam = step([*operands, jnp.asarray(rotary_table()), *states])
    weight_t, gain, wm, wf, ws, gm, gf, gs = unpack(gathered, adam, width)
    return (
        wm, wf, ws, gm.reshape(OWN), gf.reshape(OWN), gs.reshape(OWN), weight_t.T, gain.reshape(width)
    )


def solution(mesh):
    both = P(("outer", "inner"), None)
    one = P(("outer", "inner"))
    return jax.shard_map(
        shards,
        mesh=mesh,
        in_specs=(both, both, both, P(), P(), both, both, both, one, one, one),
        out_specs=(both, both, both, one, one, one, P(), P()),
        check_vma=False,
    )
```

```python
import functools

import jax
import jax.numpy as jnp
import numpy as np
from jax import lax
from jax.experimental import pallas as pl
from jax.experimental.pallas import tpu as pltpu
from jax.sharding import PartitionSpec as P

STEP = 20
beta_one = 0.9
beta_two = 0.95
learning_rate = 0.00022
adam_epsilon = 1e-08
norm_epsilon = 1e-06

MESH = pl.DeviceIdType.MESH
F32 = jnp.float32
BF16 = jnp.bfloat16
ROPE = 64
HALF = ROPE // 2
OWN = 7
LANES = 128
BLOCK = OWN * LANES

NC, NX, NY, NZL, NZH = 2, 4, 4, 8, 4
NEAR = 4
FAR = NZL * NZH // NEAR
SPAN = NZL // NEAR
ROWS = 48


def rotary_table():
    frequency = 10000.0 ** (-np.arange(HALF) / HALF)
    angles = frequency[:, None] * np.arange(LANES)[None, :]
    return np.concatenate([np.cos(angles), np.sin(angles)]).astype(np.float32)


def iota(shape, axis):
    return lax.broadcasted_iota(jnp.int32, shape, axis)


def look_up(table, index):
    rows = [
        jnp.take_along_axis(table[8 * i : 8 * i + 8], index, axis=1)
        for i in range(table.shape[0] // 8)
    ]
    return jnp.concatenate(rows, axis=0)


def pack_shard(states):
    weight_ref, gain_ref = states
    gains = jnp.concatenate([gain_ref[...], jnp.zeros((1, ROPE - OWN), F32)], axis=1)
    rows = []
    for p in range(4):
        right = weight_ref[2 * p + 1 : 2 * p + 2, :] if p < 3 else gains
        rows.append(jnp.concatenate([weight_ref[2 * p : 2 * p + 1, :], right], axis=1))
    return rows


def latent_pair(seg_ref, key_ref, table_ref, segs, inverse_rms, tokens):
    padded = 2 * LANES
    segs[...] = jnp.full((8, padded), -1, jnp.int32)
    segs[:, :tokens] = jnp.broadcast_to(seg_ref[...], (8, tokens))
    ids = segs[...]
    lane = iota((8, padded), 1)
    begins = jnp.logical_or(ids != pltpu.roll(ids, 1, axis=1), lane == 0)
    start = jnp.where(begins, lane, 0)
    shift = 1
    while shift < padded:
        before = pltpu.roll(start, shift, axis=1)
        start = jnp.maximum(start, jnp.where(lane >= shift, before, 0))
        shift *= 2
    place = jnp.clip(lane - start, 0, LANES - 1)
    halves = [
        look_up(table_ref[...], place[:, i * LANES : (i + 1) * LANES]) for i in range(2)
    ]
    table = jnp.concatenate(halves, axis=1)[:, :tokens]
    cosine, sine = table[:HALF], table[HALF:]
    key = key_ref[...].astype(F32)
    a, b = key[:HALF], key[HALF:]
    latent = jnp.concatenate([a * cosine + b * sine, b * cosine - a * sine], axis=0)
    latent = latent.astype(BF16).astype(F32) * inverse_rms()
    high = latent.astype(BF16)
    low = (latent - high.astype(F32)).astype(BF16)
    return jnp.concatenate([high, low], axis=0)


def gradient_block(both, hidden, weight, gain_rows, wide):
    row8 = iota((8, LANES), 0)
    lane8 = iota((8, LANES), 1)
    left = iota((LANES, LANES), 1) < ROPE
    upper = iota((16, 8, LANES), 1) < 4
    product = jnp.dot(both, hidden, preferred_element_type=F32)
    product = product[:ROPE] + product[ROPE:]
    for i in range(OWN):
        part = product[:, i * LANES : (i + 1) * LANES]
        w = weight[:, i * LANES : (i + 1) * LANES].astype(F32)
        gain_grad = jnp.sum(w * part, axis=0, keepdims=True)
        chosen = row8 == lax.rem(lane8 + i * LANES, OWN)
        block = jnp.concatenate(
            [
                part * gain_rows(i),
                jnp.where(chosen, gain_grad, 0.0),
                jnp.zeros((LANES - ROPE - 8, LANES), F32),
            ],
            axis=0,
        )
        wide[i * LANES : (i + 1) * LANES, :] = block.T
    rows = [wide[pl.ds(r, LANES, stride=OWN), :] for r in range(OWN)]
    total = rows[0]
    for r in range(1, OWN):
        total = total + rows[r]
    tiles = [
        jnp.where(left, rows[2 * p], pltpu.roll(rows[2 * p + 1], ROPE, axis=1))
        for p in range(3)
    ]
    tiles.append(jnp.where(left, rows[6], total))
    tiles = [t.reshape(16, 8, LANES) for t in tiles]
    even, odd = [], []
    for one, two in ((tiles[0], tiles[1]), (tiles[2], tiles[3])):
        even.append(jnp.where(upper, one, pltpu.roll(two, 4, axis=1)))
        odd.append(jnp.where(upper, pltpu.roll(one, 4, axis=1), two))
    even = jnp.concatenate(even, axis=1).astype(BF16)
    odd = jnp.concatenate(odd, axis=1).astype(BF16)
    return even, odd


def unpack_block(tiles_ref, wide, weight_ref, gains_ref, k):
    upper = iota((16, 8, LANES), 1) < 4
    lane = iota((LANES, LANES), 1)
    even, odd = [], []
    for q in range(16):
        x, core, y = q // 4, (q // 2) % 2, 2 * (q % 2)
        even.append(tiles_ref[core, x, y].astype(F32).reshape(1, 16, LANES))
        odd.append(tiles_ref[core, x, y + 1].astype(F32).reshape(1, 16, LANES))
    even, odd = jnp.concatenate(even, axis=0), jnp.concatenate(odd, axis=0)
    tiles = []
    for i in range(2):
        e, o = even[:, 8 * i : 8 * i + 8], odd[:, 8 * i : 8 * i + 8]
        tiles.append(jnp.where(upper, e, pltpu.roll(o, 4, axis=1)))
        tiles.append(jnp.where(upper, pltpu.roll(e, 4, axis=1), o))
    tiles = [t.reshape(LANES, LANES) for t in tiles]
    for r in range(OWN):
        tile = tiles[r // 2]
        if r % 2:
            tile = pltpu.roll(tile, ROPE, axis=1)
        gain = jnp.where(lane == ROPE + r, tiles[3], 0.0)
        wide[pl.ds(r, LANES, stride=OWN), :] = jnp.where(lane < ROPE, tile, gain)
    for i in range(OWN):
        at = OWN * k + i
        block = wide[i * LANES : (i + 1) * LANES, :].T
        columns = pl.ds(pl.multiple_of(at * LANES, LANES), LANES)
        weight_ref[:, columns] = block[:ROPE].astype(BF16)
        gains_ref[pl.ds(at, 1), :] = jnp.sum(block[ROPE : ROPE + 8], axis=0, keepdims=True)


def adamw(master, first, second, gradient, decay):
    first_new = beta_one * first + (1.0 - beta_one) * gradient
    second_new = beta_two * second + (1.0 - beta_two) * gradient * gradient
    correct_one = 1.0 - beta_one ** (STEP + 1)
    correct_two = 1.0 - beta_two ** (STEP + 1)
    direction = first_new / correct_one / (jnp.sqrt(second_new / correct_two) + adam_epsilon)
    master_new = master - learning_rate * (direction + decay * master)
    return (master_new, first_new, second_new)


def step_kernel(
    hidden_hbm, seg_hbm, key_hbm, weight_hbm, gain_hbm, table_hbm,
    wm_hbm, wf_hbm, ws_hbm, gm_hbm, gf_hbm, gs_hbm,
    o0, o1, o2, o3, o4, o5, o6, o7,
    gathered_ref, new_ref, low, hidden_ref, seg_ref, key_ref, weight_ref, gain_ref, table_ref,
    wm_ref, wf_ref, ws_ref, gm_ref, gf_ref, gs_ref,
    squares, wide, segs, gains, packed_ref, shard_ref,
    r1, sb, r2, zb, r3, hb, r4, mine, shards, masters, sums, in_sem, row_sem, met, out_sem,
    s1, t1, s2, t2, s3, t3, s4, t4, s5, t5, s6, t6, s7, t7, s8, t8,
):
    tokens, width = hidden_ref.shape
    outs = (o0, o1, o2, o3, o4, o5, o6, o7)
    parts = tokens // ROWS
    outer, inner = lax.axis_index("outer"), lax.axis_index("inner")
    core, x = lax.rem(outer, NC), lax.rem(outer // NC, NX)
    y, z = inner // NZH, lax.rem(inner, NZH) * NZL + outer // (NC * NX)
    near, far = lax.rem(z, NEAR), z // NEAR

    def device(x=x, y=y, near=near, far=far, core=core):
        z = far * NEAR + near
        return ((lax.rem(z, NZL) * NX + x) * NC + core, y * NZH + z // NZL)

    loads = [
        pltpu.make_async_copy(src, dst, in_sem.at[i])
        for i, (src, dst) in enumerate(
            (
                (seg_hbm, seg_ref), (key_hbm, key_ref), (table_hbm, table_ref),
                (gain_hbm, gain_ref), (weight_hbm, weight_ref),
                (wm_hbm, wm_ref), (wf_hbm, wf_ref), (ws_hbm, ws_ref),
                (gm_hbm, gm_ref), (gf_hbm, gf_ref), (gs_hbm, gs_ref),
            )
        )
    ]

    def part_of_hidden(i):
        rows = pl.ds(pl.multiple_of(i * ROWS, 16), ROWS)
        return pltpu.make_async_copy(hidden_hbm.at[rows], hidden_ref.at[rows], row_sem.at[i])

    for load in loads[:4]:
        load.start()
    for i in range(parts):
        part_of_hidden(i).start()
    for load in loads[4:]:
        load.start()

    sibling = device(core=1 - core)
    order_x = sorted(range(NX), key=lambda d: (d == 0, -min(d, NX - d)))
    order_y = sorted(range(NY), key=lambda d: -min(d, NY - d))
    plane = [(dx, dy) for dx in order_x for dy in order_y]
    others = [o for o in plane if o != (0, 0)]
    ahead = {o: (lax.rem(x + o[0], NX), lax.rem(y + o[1], NY)) for o in plane}
    behind = {o: (lax.rem(x + NX - o[0], NX), lax.rem(y + NY - o[1], NY)) for o in plane}
    up_near = [lax.rem(near + d, NEAR) for d in range(NEAR)]
    quarters = [up_near[(t + 1) % NEAR] for t in range(NEAR)]
    behind_near = [lax.rem(near + NEAR - d, NEAR) for d in range(NEAR)]
    up_far = [lax.rem(far + d, FAR) for d in range(FAR)]
    far_first = sorted(range(1, FAR), key=lambda d: -min(d, FAR - d))

    barrier = pltpu.get_barrier_semaphore()
    reach = [1 << i for i in range((FAR // 2).bit_length() - 1)]
    steps = [[device(far=up_far[d]), device(far=up_far[FAR - d])] for d in reach]
    peers = list(steps[0])
    peers += [device(near=n) for n in up_near[1:]]
    peers += [device(x=ahead[o][0], y=ahead[o][1]) for o in others]
    peers += [sibling]
    for peer in peers:
        pl.semaphore_signal(barrier, inc=1, device_id=peer, device_id_type=MESH)

    def send(src, dst, s, t, to):
        copy = pltpu.make_async_remote_copy(
            src_ref=src, dst_ref=dst, send_sem=s, recv_sem=t, device_id=to, device_id_type=MESH
        )
        copy.start()
        return copy

    squares[tokens:, :] = jnp.zeros((2 * LANES - tokens, LANES), F32)

    def square(i, carry):
        part_of_hidden(i).wait()
        rows = pl.ds(pl.multiple_of(i * ROWS, 16), ROWS)
        total = jnp.zeros((ROWS, LANES), F32)
        for j in range(width // LANES):
            h = hidden_ref[rows, j * LANES : (j + 1) * LANES].astype(F32)
            total = total + h * h
        squares[rows, :] = total
        return carry

    def inverse_rms():
        lax.fori_loop(0, parts, square, 0)
        mean = jnp.sum(squares[...].T, axis=0, keepdims=True) * (1.0 / width)
        return lax.rsqrt(mean + norm_epsilon)[:, :tokens]

    for load in loads[:3]:
        load.wait()
    both = latent_pair(seg_ref, key_ref, table_ref, segs, inverse_rms, tokens)
    for load in loads[3:5]:
        load.wait()
    gains[...] = gain_ref[...].astype(F32)

    pl.semaphore_wait(barrier, len(peers))
    for peer in steps[0]:
        pl.semaphore_signal(met.at[0], inc=1, device_id=peer, device_id_type=MESH)

    def gradients(t):
        n = quarters[t]
        for h in range(SPAN):
            k = h * NEAR + n
            columns = pl.ds(pl.multiple_of(k * BLOCK, LANES), BLOCK)
            even, odd = gradient_block(
                both, hidden_ref[:, columns], weight_ref[:, columns],
                lambda i: gains[pl.ds(OWN * k + i, 1), :], wide.at[h],
            )
            for q in range(16):
                xq, cq, yq = q // 4, (q // 2) % 2, 2 * (q % 2)
                packed_ref[t, cq, xq, yq, h] = even[q]
                packed_ref[t, cq, xq, yq + 1, h] = odd[q]

    def halves(t):
        return send(packed_ref.at[t, 1 - core], r1.at[t], s1.at[t], t1.at[t], sibling)

    def to_plane(t):
        first[t].wait_recv()
        sb[t] = (packed_ref[t, core].astype(F32) + r1[t].astype(F32)).astype(BF16)
        for i, o in enumerate(others):
            xs, ys = ahead[o]
            send(sb.at[t, xs, ys], r2.at[t, i], s2, t2.at[t], device(x=xs, y=ys))

    first = []
    for t in range(NEAR):
        gradients(t)
        first.append(halves(t))
        if t > 0:
            to_plane(t - 1)
        if t == NEAR - 1:
            for i in range(1, len(steps)):
                pl.semaphore_wait(met.at[i - 1], 2)
                for peer in steps[i]:
                    pl.semaphore_signal(met.at[i], inc=1, device_id=peer, device_id_type=MESH)

    for load in loads[5:]:
        load.wait()
    for a, states in enumerate(((wm_ref, gm_ref), (wf_ref, gf_ref), (ws_ref, gs_ref))):
        for p, row in enumerate(pack_shard(states)):
            shard_ref[4 * a + p : 4 * a + p + 1, :] = row
    shard = shard_ref[0:12, :]
    master = shard[0:4].astype(BF16).astype(F32)
    mine[...] = jnp.concatenate([master, shard[0:4] - master, shard[4:12]], axis=0).astype(BF16)

    to_plane(NEAR - 1)

    third = []
    for t in range(NEAR):
        pltpu.make_async_copy(r2.at[t], r2.at[t], t2.at[t]).wait()
        total = sb[t, x, y].astype(F32)
        for i in range(len(others)):
            total = total + r2[t, i].astype(F32)
        if t < NEAR - 1:
            zb[t] = total.astype(BF16)
            third.append(
                send(zb.at[t], r3.at[t], s3.at[t], t3.at[t], device(near=quarters[t]))
            )
        if t == 0:
            pl.semaphore_wait(met.at[len(steps) - 1], 2)
            swaps = [
                send(mine, shards.at[far], s8.at[d], t8.at[d], device(far=up_far[d]))
                for d in far_first
            ]
            shards[far] = mine[...]
    for t in range(NEAR - 1):
        third[t].wait_recv()
        total = total + r3[t].astype(F32)
    hb[...] = total.astype(BF16)

    fourth = [
        send(hb, r4.at[far], s4.at[d], t4.at[d], device(far=up_far[d])) for d in far_first
    ]
    r4[far] = hb[...]
    for c in first + third:
        c.wait_send()
    pltpu.make_async_copy(r2, r2, s2).wait()

    for c in swaps:
        c.wait_recv()
    for f in range(FAR):
        state = shards[f].astype(F32)
        state = [state[0:4] + state[4:8], state[8:12], state[12:16]]
        for a in range(3):
            for p in range(4):
                row = p * NZH + f // SPAN
                masters[a, f % SPAN, row : row + 1, :] = state[a][p : p + 1]

    for c in fourth:
        c.wait_recv()
    gradient = r4[0].astype(F32)
    for f in range(1, FAR):
        gradient = gradient + r4[f].astype(F32)

    tile = gradient.shape
    is_gain = jnp.logical_and(iota(tile, 1) >= 3 * NZH, iota(tile, 2) >= ROPE)
    decay = jnp.where(is_gain, 0.0, 0.1)
    new = adamw(masters[0], masters[1], masters[2], gradient, decay)

    own = gathered_ref.at[core, :, x, y]
    gathered_ref[core, 0, x, y] = new[0].astype(BF16)
    fifth = [
        send(own.at[0], own.at[d], s5.at[d], t5.at[d], device(near=up_near[d]))
        for d in range(1, NEAR)
    ]

    sums[...] = gradient
    zh = z // NZL
    gradient = [sums[lax.rem(far, SPAN), pl.ds(p * NZH + zh, 1), :] for p in range(4)]
    is_gain = jnp.logical_and(iota((4, LANES), 0) == 3, iota((4, LANES), 1) >= ROPE)
    decay = jnp.where(is_gain, 0.0, 0.1)
    shard = shard_ref[0:12, :]
    new = adamw(shard[0:4], shard[4:8], shard[8:12], jnp.concatenate(gradient, axis=0), decay)
    for a, (w, g) in enumerate(((wm_ref, gm_ref), (wf_ref, gf_ref), (ws_ref, gs_ref))):
        for p in range(4):
            row = new[a][p : p + 1]
            w[2 * p : 2 * p + 1, :] = row[:, :ROPE]
            if p < 3:
                w[2 * p + 1 : 2 * p + 2, :] = row[:, ROPE:]
            else:
                g[...] = row[:, ROPE : ROPE + OWN]
    out = [
        pltpu.make_async_copy(src, dst, out_sem.at[i])
        for i, (src, dst) in enumerate(
            zip((wm_ref, wf_ref, ws_ref, gm_ref, gf_ref, gs_ref), outs[2:], strict=True)
        )
    ]
    for c in out:
        c.start()
    for c in swaps + fourth:
        c.wait_send()

    for d in range(NEAR):
        if d > 0:
            fifth[d - 1].wait_recv()
        for o in others:
            send(own.at[d], own.at[d], s6, t6.at[d], device(x=ahead[o][0], y=ahead[o][1]))
    for c in fifth:
        c.wait_send()

    def whole(d):
        part = gathered_ref.at[1 - core, d]
        pltpu.make_async_copy(part, part, t7.at[d]).wait()
        for h in range(SPAN):
            k = h * NEAR + behind_near[d]
            unpack_block(gathered_ref.at[:, d, :, :, h], wide.at[h], new_ref, gains, k)
            columns = pl.ds(pl.multiple_of(k * BLOCK, LANES), BLOCK)
            out.append(
                pltpu.make_async_copy(
                    new_ref.at[:, columns], outs[0].at[:, columns], out_sem.at[len(out)]
                )
            )
            out[-1].start()

    for d in range(NEAR):
        pltpu.make_async_copy(r2.at[d], r2.at[d], t6.at[d]).wait()
        part = gathered_ref.at[core, d]
        send(part, part, s7, t7.at[d], sibling)
        if d > 0:
            whole(d - 1)
    whole(NEAR - 1)
    low[...] = gains[...].astype(BF16)
    out.append(pltpu.make_async_copy(low, outs[1], out_sem.at[len(out)]))
    out[-1].start()
    pltpu.make_async_copy(r2, r2, s6).wait()
    half = gathered_ref.at[0]
    pltpu.make_async_copy(half, half, s7).wait()
    for c in out:
        c.wait()


def copy_kernel(n, *refs):
    src, dst, by, (sem_in, sem_out) = refs[:n], refs[n : 2 * n], refs[2 * n : 3 * n], refs[3 * n :]
    rows = [pl.ds(16 * i, 16) for i in range(src[0].shape[0] // 16)]
    ways = [tuple(ref[0].at[r] for ref in (src, by, dst)) for r in rows]
    ways += list(zip(src[1:], by[1:], dst[1:], strict=True))
    copies_in = [pltpu.make_async_copy(a, b, sem_in.at[i]) for i, (a, b, _) in enumerate(ways)]
    copies_out = [pltpu.make_async_copy(b, c, sem_out.at[i]) for i, (_, b, c) in enumerate(ways)]
    for c in copies_in:
        c.start()
    for c, after in zip(copies_in, copies_out, strict=True):
        c.wait()
        after.start()
    for c in copies_out:
        c.wait()


def results(width):
    items = [((ROPE, width), BF16), ((width // LANES, LANES), BF16)]
    items += [((OWN, ROPE), F32)] * 3 + [((1, OWN), F32)] * 3
    return [jax.ShapeDtypeStruct(s, t) for s, t in items]


def step(operands):
    hidden = operands[0]
    tokens, width = hidden.shape
    dma = pltpu.SemaphoreType.DMA
    piece = (SPAN, 16, LANES)
    others = NX * NY - 1
    chunk = (NEAR, *piece)
    counts = [NEAR, NEAR, 0, NEAR, NEAR, NEAR, FAR, FAR, NEAR, NEAR, 0, NEAR, 0, NEAR, FAR, FAR]
    return pl.pallas_call(
        step_kernel,
        out_shape=results(width),
        in_specs=[pl.BlockSpec(memory_space=pltpu.HBM)] * len(operands),
        out_specs=[pl.BlockSpec(memory_space=pltpu.HBM)] * 8,
        scratch_shapes=[
            pltpu.VMEM((NC, NEAR, NX, NY, *piece), BF16),
            pltpu.VMEM((ROPE, width), BF16),
            pltpu.VMEM((width // LANES, LANES), BF16),
        ]
        + [pltpu.VMEM(o.shape, o.dtype) for o in operands]
        + [
            pltpu.VMEM((2 * LANES, LANES), F32),
            pltpu.VMEM((SPAN, BLOCK, LANES), F32),
            pltpu.VMEM((8, 2 * LANES), jnp.int32),
            pltpu.VMEM((width // LANES, LANES), F32),
            pltpu.VMEM((NEAR, NC, NX, NY, *piece), BF16),
            pltpu.VMEM((16, LANES), F32),
            pltpu.VMEM((NEAR, NX, NY, *piece), BF16),
            pltpu.VMEM((NEAR, NX, NY, *piece), BF16),
            pltpu.VMEM((NEAR, others, *piece), BF16),
            pltpu.VMEM(chunk, BF16),
            pltpu.VMEM(chunk, BF16),
            pltpu.VMEM(piece, BF16),
            pltpu.VMEM((FAR, *piece), BF16),
            pltpu.VMEM((16, LANES), BF16),
            pltpu.VMEM((FAR, 16, LANES), BF16),
            pltpu.VMEM((3, *piece), F32),
            pltpu.VMEM(piece, F32),
            dma((len(operands) - 1,)),
            dma((tokens // ROWS,)),
            pltpu.SemaphoreType.REGULAR((2,)),
            dma((6 + NZL + 1,)),
        ]
        + [dma((n,)) if n else dma for n in counts],
        compiler_params=pltpu.CompilerParams(
            collective_id=0, has_side_effects=True, vmem_limit_bytes=56 * 1024 * 1024
        ),
    )(*operands)


def hand_on(arrays):
    hbm = [pl.BlockSpec(memory_space=pltpu.HBM)] * len(arrays)
    copies = arrays[0].shape[0] // 16 + len(arrays) - 1
    return pl.pallas_call(
        functools.partial(copy_kernel, len(arrays)),
        out_shape=[jax.ShapeDtypeStruct(a.shape, a.dtype) for a in arrays],
        in_specs=hbm,
        out_specs=hbm,
        scratch_shapes=[pltpu.VMEM(a.shape, a.dtype) for a in arrays]
        + [pltpu.SemaphoreType.DMA((copies,))] * 2,
        compiler_params=pltpu.CompilerParams(vmem_limit_bytes=56 * 1024 * 1024),
    )(*arrays)


def shards(
    hidden, segment_ids, key_grad, weight_bf16, gain_bf16,
    weight_master, weight_first, weight_second, gain_master, gain_first, gain_second,
):
    width = hidden.shape[1]
    states = [weight_master, weight_first, weight_second]
    states += [g.reshape(1, OWN) for g in (gain_master, gain_first, gain_second)]
    operands = [hidden, segment_ids, key_grad.T, weight_bf16.T, gain_bf16.reshape(width // LANES, LANES)]
    arrays = step([*operands, jnp.asarray(rotary_table()), *states])
    weight_t, gain, wm, wf, ws, gm, gf, gs = hand_on(arrays)
    return (
        wm, wf, ws, gm.reshape(OWN), gf.reshape(OWN), gs.reshape(OWN), weight_t.T, gain.reshape(width)
    )


def solution(mesh):
    both = P(("outer", "inner"), None)
    one = P(("outer", "inner"))
    return jax.shard_map(
        shards,
        mesh=mesh,
        in_specs=(both, both, both, P(), P(), both, both, both, one, one, one),
        out_specs=(both, both, both, one, one, one, P(), P()),
        check_vma=False,
    )
```

```python
import functools

import jax
import jax.numpy as jnp
import numpy as np
from jax import lax
from jax.experimental import pallas as pl
from jax.experimental.pallas import tpu as pltpu
from jax.sharding import PartitionSpec as P

STEP = 20
beta_one = 0.9
beta_two = 0.95
learning_rate = 0.00022
adam_epsilon = 1e-08
norm_epsilon = 1e-06

MESH = pl.DeviceIdType.MESH
F32 = jnp.float32
BF16 = jnp.bfloat16
ROPE = 64
HALF = ROPE // 2
OWN = 7
LANES = 128
BLOCK = OWN * LANES

NC, NX, NY, NZL, NZH = 2, 4, 4, 8, 4
NEAR = 4
FAR = NZL * NZH // NEAR
SPAN = NZL // NEAR
ROWS = 48


def rotary_table():
    frequency = 10000.0 ** (-np.arange(HALF) / HALF)
    angles = frequency[:, None] * np.arange(LANES)[None, :]
    return np.concatenate([np.cos(angles), np.sin(angles)]).astype(np.float32)


def iota(shape, axis):
    return lax.broadcasted_iota(jnp.int32, shape, axis)


def look_up(table, index):
    rows = [
        jnp.take_along_axis(table[8 * i : 8 * i + 8], index, axis=1)
        for i in range(table.shape[0] // 8)
    ]
    return jnp.concatenate(rows, axis=0)


def pack_shard(states):
    weight_ref, gain_ref = states
    gains = jnp.concatenate([gain_ref[...], jnp.zeros((1, ROPE - OWN), F32)], axis=1)
    rows = []
    for p in range(4):
        right = weight_ref[2 * p + 1 : 2 * p + 2, :] if p < 3 else gains
        rows.append(jnp.concatenate([weight_ref[2 * p : 2 * p + 1, :], right], axis=1))
    return rows


def latent_pair(seg_ref, key_ref, table_ref, segs, inverse_rms, tokens):
    padded = 2 * LANES
    segs[...] = jnp.full((8, padded), -1, jnp.int32)
    segs[:, :tokens] = jnp.broadcast_to(seg_ref[...], (8, tokens))
    ids = segs[...]
    lane = iota((8, padded), 1)
    begins = jnp.logical_or(ids != pltpu.roll(ids, 1, axis=1), lane == 0)
    start = jnp.where(begins, lane, 0)
    shift = 1
    while shift < padded:
        before = pltpu.roll(start, shift, axis=1)
        start = jnp.maximum(start, jnp.where(lane >= shift, before, 0))
        shift *= 2
    place = jnp.clip(lane - start, 0, LANES - 1)
    halves = [
        look_up(table_ref[...], place[:, i * LANES : (i + 1) * LANES]) for i in range(2)
    ]
    table = jnp.concatenate(halves, axis=1)[:, :tokens]
    cosine, sine = table[:HALF], table[HALF:]
    key = key_ref[...].astype(F32)
    a, b = key[:HALF], key[HALF:]
    latent = jnp.concatenate([a * cosine + b * sine, b * cosine - a * sine], axis=0)
    latent = latent.astype(BF16).astype(F32) * inverse_rms()
    high = latent.astype(BF16)
    low = (latent - high.astype(F32)).astype(BF16)
    return jnp.concatenate([high, low], axis=0)


def gradient_block(both, hidden, weight, gain_rows, wide):
    row8 = iota((8, LANES), 0)
    lane8 = iota((8, LANES), 1)
    left = iota((LANES, LANES), 1) < ROPE
    upper = iota((16, 8, LANES), 1) < 4
    product = jnp.dot(both, hidden, preferred_element_type=F32)
    product = product[:ROPE] + product[ROPE:]
    for i in range(OWN):
        part = product[:, i * LANES : (i + 1) * LANES]
        w = weight[:, i * LANES : (i + 1) * LANES].astype(F32)
        gain_grad = jnp.sum(w * part, axis=0, keepdims=True)
        chosen = row8 == lax.rem(lane8 + i * LANES, OWN)
        block = jnp.concatenate(
            [
                part * gain_rows(i),
                jnp.where(chosen, gain_grad, 0.0),
                jnp.zeros((LANES - ROPE - 8, LANES), F32),
            ],
            axis=0,
        )
        wide[i * LANES : (i + 1) * LANES, :] = block.T
    rows = [wide[pl.ds(r, LANES, stride=OWN), :] for r in range(OWN)]
    total = rows[0]
    for r in range(1, OWN):
        total = total + rows[r]
    tiles = [
        jnp.where(left, rows[2 * p], pltpu.roll(rows[2 * p + 1], ROPE, axis=1))
        for p in range(3)
    ]
    tiles.append(jnp.where(left, rows[6], total))
    tiles = [t.reshape(16, 8, LANES) for t in tiles]
    even, odd = [], []
    for one, two in ((tiles[0], tiles[1]), (tiles[2], tiles[3])):
        even.append(jnp.where(upper, one, pltpu.roll(two, 4, axis=1)))
        odd.append(jnp.where(upper, pltpu.roll(one, 4, axis=1), two))
    even = jnp.concatenate(even, axis=1).astype(BF16)
    odd = jnp.concatenate(odd, axis=1).astype(BF16)
    return even, odd


def unpack_block(tiles_ref, wide, weight_ref, gains_ref, k):
    upper = iota((16, 8, LANES), 1) < 4
    lane = iota((LANES, LANES), 1)
    even, odd = [], []
    for q in range(16):
        x, core, y = q // 4, (q // 2) % 2, 2 * (q % 2)
        even.append(tiles_ref[core, x, y].astype(F32).reshape(1, 16, LANES))
        odd.append(tiles_ref[core, x, y + 1].astype(F32).reshape(1, 16, LANES))
    even, odd = jnp.concatenate(even, axis=0), jnp.concatenate(odd, axis=0)
    tiles = []
    for i in range(2):
        e, o = even[:, 8 * i : 8 * i + 8], odd[:, 8 * i : 8 * i + 8]
        tiles.append(jnp.where(upper, e, pltpu.roll(o, 4, axis=1)))
        tiles.append(jnp.where(upper, pltpu.roll(e, 4, axis=1), o))
    tiles = [t.reshape(LANES, LANES) for t in tiles]
    for r in range(OWN):
        tile = tiles[r // 2]
        if r % 2:
            tile = pltpu.roll(tile, ROPE, axis=1)
        gain = jnp.where(lane == ROPE + r, tiles[3], 0.0)
        wide[pl.ds(r, LANES, stride=OWN), :] = jnp.where(lane < ROPE, tile, gain)
    for i in range(OWN):
        at = OWN * k + i
        block = wide[i * LANES : (i + 1) * LANES, :].T
        columns = pl.ds(pl.multiple_of(at * LANES, LANES), LANES)
        weight_ref[:, columns] = block[:ROPE].astype(BF16)
        gains_ref[pl.ds(at, 1), :] = jnp.sum(block[ROPE : ROPE + 8], axis=0, keepdims=True)


def adamw(master, first, second, gradient, decay):
    first_new = beta_one * first + (1.0 - beta_one) * gradient
    second_new = beta_two * second + (1.0 - beta_two) * gradient * gradient
    correct_one = 1.0 - beta_one ** (STEP + 1)
    correct_two = 1.0 - beta_two ** (STEP + 1)
    direction = first_new / correct_one / (jnp.sqrt(second_new / correct_two) + adam_epsilon)
    master_new = master - learning_rate * (direction + decay * master)
    return (master_new, first_new, second_new)


def step_kernel(
    hidden_hbm, seg_hbm, key_hbm, weight_hbm, gain_hbm, table_hbm,
    wm_hbm, wf_hbm, ws_hbm, gm_hbm, gf_hbm, gs_hbm,
    o0, o1, o2, o3, o4, o5, o6, o7,
    gathered_ref, new_ref, low, hidden_ref, seg_ref, key_ref, weight_ref, gain_ref, table_ref,
    wm_ref, wf_ref, ws_ref, gm_ref, gf_ref, gs_ref,
    squares, wide, segs, gains, packed_ref, shard_ref,
    r1, sb, r2, zb, r3, hb, r4, mine, shards, masters, sums, in_sem, row_sem, met, out_sem,
    s1, t1, s2, t2, s3, t3, s4, t4, s5, t5, s6, t6, s7, t7, s8, t8,
):
    tokens, width = hidden_ref.shape
    outs = (o0, o1, o2, o3, o4, o5, o6, o7)
    parts = tokens // ROWS
    outer, inner = lax.axis_index("outer"), lax.axis_index("inner")
    core, x = lax.rem(outer, NC), lax.rem(outer // NC, NX)
    y, z = inner // NZH, lax.rem(inner, NZH) * NZL + outer // (NC * NX)
    near, far = lax.rem(z, NEAR), z // NEAR

    def device(x=x, y=y, near=near, far=far, core=core):
        z = far * NEAR + near
        return ((lax.rem(z, NZL) * NX + x) * NC + core, y * NZH + z // NZL)

    loads = [
        pltpu.make_async_copy(src, dst, in_sem.at[i])
        for i, (src, dst) in enumerate(
            (
                (seg_hbm, seg_ref), (key_hbm, key_ref), (table_hbm, table_ref),
                (gain_hbm, gain_ref), (weight_hbm, weight_ref),
                (wm_hbm, wm_ref), (wf_hbm, wf_ref), (ws_hbm, ws_ref),
                (gm_hbm, gm_ref), (gf_hbm, gf_ref), (gs_hbm, gs_ref),
            )
        )
    ]

    def part_of_hidden(i):
        rows = pl.ds(pl.multiple_of(i * ROWS, 16), ROWS)
        return pltpu.make_async_copy(hidden_hbm.at[rows], hidden_ref.at[rows], row_sem.at[i])

    for load in loads[:4]:
        load.start()
    for i in range(parts):
        part_of_hidden(i).start()
    for load in loads[4:]:
        load.start()

    sibling = device(core=1 - core)
    order_x = sorted(range(NX), key=lambda d: (d == 0, -min(d, NX - d)))
    order_y = sorted(range(NY), key=lambda d: -min(d, NY - d))
    plane = [(dx, dy) for dx in order_x for dy in order_y]
    others = [o for o in plane if o != (0, 0)]
    ahead = {o: (lax.rem(x + o[0], NX), lax.rem(y + o[1], NY)) for o in plane}
    behind = {o: (lax.rem(x + NX - o[0], NX), lax.rem(y + NY - o[1], NY)) for o in plane}
    up_near = [lax.rem(near + d, NEAR) for d in range(NEAR)]
    quarters = [up_near[(t + 1) % NEAR] for t in range(NEAR)]
    behind_near = [lax.rem(near + NEAR - d, NEAR) for d in range(NEAR)]
    up_far = [lax.rem(far + d, FAR) for d in range(FAR)]
    far_first = sorted(range(1, FAR), key=lambda d: -min(d, FAR - d))

    barrier = pltpu.get_barrier_semaphore()
    reach = [1 << i for i in range((FAR // 2).bit_length() - 1)]
    steps = [[device(far=up_far[d]), device(far=up_far[FAR - d])] for d in reach]
    peers = list(steps[0])
    peers += [device(near=n) for n in up_near[1:]]
    peers += [device(x=ahead[o][0], y=ahead[o][1]) for o in others]
    peers += [sibling]
    for peer in peers:
        pl.semaphore_signal(barrier, inc=1, device_id=peer, device_id_type=MESH)

    def send(src, dst, s, t, to):
        copy = pltpu.make_async_remote_copy(
            src_ref=src, dst_ref=dst, send_sem=s, recv_sem=t, device_id=to, device_id_type=MESH
        )
        copy.start()
        return copy

    squares[tokens:, :] = jnp.zeros((2 * LANES - tokens, LANES), F32)

    def square(i, carry):
        part_of_hidden(i).wait()
        rows = pl.ds(pl.multiple_of(i * ROWS, 16), ROWS)
        total = jnp.zeros((ROWS, LANES), F32)
        for j in range(width // LANES):
            h = hidden_ref[rows, j * LANES : (j + 1) * LANES].astype(F32)
            total = total + h * h
        squares[rows, :] = total
        return carry

    def inverse_rms():
        lax.fori_loop(0, parts, square, 0)
        mean = jnp.sum(squares[...].T, axis=0, keepdims=True) * (1.0 / width)
        return lax.rsqrt(mean + norm_epsilon)[:, :tokens]

    for load in loads[:3]:
        load.wait()
    both = latent_pair(seg_ref, key_ref, table_ref, segs, inverse_rms, tokens)
    for load in loads[3:5]:
        load.wait()
    gains[...] = gain_ref[...].astype(F32)

    pl.semaphore_wait(barrier, len(peers))
    for peer in steps[0]:
        pl.semaphore_signal(met.at[0], inc=1, device_id=peer, device_id_type=MESH)

    def gradients(t):
        n = quarters[t]
        for h in range(SPAN):
            k = h * NEAR + n
            columns = pl.ds(pl.multiple_of(k * BLOCK, LANES), BLOCK)
            even, odd = gradient_block(
                both, hidden_ref[:, columns], weight_ref[:, columns],
                lambda i: gains[pl.ds(OWN * k + i, 1), :], wide.at[h],
            )
            for q in range(16):
                xq, cq, yq = q // 4, (q // 2) % 2, 2 * (q % 2)
                packed_ref[t, cq, xq, yq, h] = even[q]
                packed_ref[t, cq, xq, yq + 1, h] = odd[q]

    def halves(t):
        return send(packed_ref.at[t, 1 - core], r1.at[t], s1.at[t], t1.at[t], sibling)

    def to_plane(t):
        first[t].wait_recv()
        sb[t] = (packed_ref[t, core].astype(F32) + r1[t].astype(F32)).astype(BF16)
        for i, o in enumerate(others):
            xs, ys = ahead[o]
            send(sb.at[t, xs, ys], r2.at[t, i], s2, t2.at[t], device(x=xs, y=ys))

    first = []
    for t in range(NEAR):
        gradients(t)
        first.append(halves(t))
        if t > 0:
            to_plane(t - 1)
        if t == NEAR - 1:
            for i in range(1, len(steps)):
                pl.semaphore_wait(met.at[i - 1], 2)
                for peer in steps[i]:
                    pl.semaphore_signal(met.at[i], inc=1, device_id=peer, device_id_type=MESH)

    for load in loads[5:]:
        load.wait()
    for a, states in enumerate(((wm_ref, gm_ref), (wf_ref, gf_ref), (ws_ref, gs_ref))):
        for p, row in enumerate(pack_shard(states)):
            shard_ref[4 * a + p : 4 * a + p + 1, :] = row
    shard = shard_ref[0:12, :]
    master = shard[0:4].astype(BF16).astype(F32)
    mine[...] = jnp.concatenate([master, shard[0:4] - master, shard[4:12]], axis=0).astype(BF16)

    to_plane(NEAR - 1)

    third = []
    for t in range(NEAR):
        pltpu.make_async_copy(r2.at[t], r2.at[t], t2.at[t]).wait()
        total = sb[t, x, y].astype(F32)
        for i in range(len(others)):
            total = total + r2[t, i].astype(F32)
        if t < NEAR - 1:
            zb[t] = total.astype(BF16)
            third.append(
                send(zb.at[t], r3.at[t], s3.at[t], t3.at[t], device(near=quarters[t]))
            )
        if t == 0:
            pl.semaphore_wait(met.at[len(steps) - 1], 2)
            swaps = [
                send(mine, shards.at[far], s8.at[d], t8.at[d], device(far=up_far[d]))
                for d in far_first
            ]
            shards[far] = mine[...]
    for t in range(NEAR - 1):
        third[t].wait_recv()
        total = total + r3[t].astype(F32)
    hb[...] = total.astype(BF16)

    fourth = [
        send(hb, r4.at[far], s4.at[d], t4.at[d], device(far=up_far[d])) for d in far_first
    ]
    r4[far] = hb[...]
    for c in first + third:
        c.wait_send()
    pltpu.make_async_copy(r2, r2, s2).wait()

    for c in swaps:
        c.wait_recv()
    for f in range(FAR):
        state = shards[f].astype(F32)
        state = [state[0:4] + state[4:8], state[8:12], state[12:16]]
        for a in range(3):
            for p in range(4):
                row = p * NZH + f // SPAN
                masters[a, f % SPAN, row : row + 1, :] = state[a][p : p + 1]

    for c in fourth:
        c.wait_recv()
    gradient = r4[0].astype(F32)
    for f in range(1, FAR):
        gradient = gradient + r4[f].astype(F32)

    tile = gradient.shape
    is_gain = jnp.logical_and(iota(tile, 1) >= 3 * NZH, iota(tile, 2) >= ROPE)
    decay = jnp.where(is_gain, 0.0, 0.1)
    new = adamw(masters[0], masters[1], masters[2], gradient, decay)

    own = gathered_ref.at[core, :, x, y]
    gathered_ref[core, 0, x, y] = new[0].astype(BF16)
    fifth = [
        send(own.at[0], own.at[d], s5.at[d], t5.at[d], device(near=up_near[d]))
        for d in range(1, NEAR)
    ]

    def to_all(d):
        for o in others:
            send(own.at[d], own.at[d], s6, t6.at[d], device(x=ahead[o][0], y=ahead[o][1]))

    to_all(0)

    sums[...] = gradient
    zh = z // NZL
    gradient = [sums[lax.rem(far, SPAN), pl.ds(p * NZH + zh, 1), :] for p in range(4)]
    is_gain = jnp.logical_and(iota((4, LANES), 0) == 3, iota((4, LANES), 1) >= ROPE)
    decay = jnp.where(is_gain, 0.0, 0.1)
    shard = shard_ref[0:12, :]
    new = adamw(shard[0:4], shard[4:8], shard[8:12], jnp.concatenate(gradient, axis=0), decay)
    for a, (w, g) in enumerate(((wm_ref, gm_ref), (wf_ref, gf_ref), (ws_ref, gs_ref))):
        for p in range(4):
            row = new[a][p : p + 1]
            w[2 * p : 2 * p + 1, :] = row[:, :ROPE]
            if p < 3:
                w[2 * p + 1 : 2 * p + 2, :] = row[:, ROPE:]
            else:
                g[...] = row[:, ROPE : ROPE + OWN]
    out = [
        pltpu.make_async_copy(src, dst, out_sem.at[i])
        for i, (src, dst) in enumerate(
            zip((wm_ref, wf_ref, ws_ref, gm_ref, gf_ref, gs_ref), outs[2:], strict=True)
        )
    ]
    for c in out:
        c.start()

    for d in range(1, NEAR):
        fifth[d - 1].wait_recv()
        to_all(d)

    def whole(d):
        part = gathered_ref.at[1 - core, d]
        pltpu.make_async_copy(part, part, t7.at[d]).wait()
        for h in range(SPAN):
            k = h * NEAR + behind_near[d]
            unpack_block(gathered_ref.at[:, d, :, :, h], wide.at[h], new_ref, gains, k)
            columns = pl.ds(pl.multiple_of(k * BLOCK, LANES), BLOCK)
            out.append(
                pltpu.make_async_copy(
                    new_ref.at[:, columns], outs[0].at[:, columns], out_sem.at[len(out)]
                )
            )
            out[-1].start()

    for d in range(NEAR):
        pltpu.make_async_copy(r2.at[d], r2.at[d], t6.at[d]).wait()
        part = gathered_ref.at[core, d]
        send(part, part, s7, t7.at[d], sibling)
        if d > 0:
            whole(d - 1)
    whole(NEAR - 1)
    low[...] = gains[...].astype(BF16)
    out.append(pltpu.make_async_copy(low, outs[1], out_sem.at[len(out)]))
    out[-1].start()
    for c in swaps + fourth + fifth:
        c.wait_send()
    pltpu.make_async_copy(r2, r2, s6).wait()
    half = gathered_ref.at[0]
    pltpu.make_async_copy(half, half, s7).wait()
    for c in out:
        c.wait()


def copy_kernel(n, *refs):
    src, dst, by, (sem_in, sem_out) = refs[:n], refs[n : 2 * n], refs[2 * n : 3 * n], refs[3 * n :]
    rows = [pl.ds(16 * i, 16) for i in range(src[0].shape[0] // 16)]
    ways = [tuple(ref[0].at[r] for ref in (src, by, dst)) for r in rows]
    ways += list(zip(src[1:], by[1:], dst[1:], strict=True))
    copies_in = [pltpu.make_async_copy(a, b, sem_in.at[i]) for i, (a, b, _) in enumerate(ways)]
    copies_out = [pltpu.make_async_copy(b, c, sem_out.at[i]) for i, (_, b, c) in enumerate(ways)]
    for c in copies_in:
        c.start()
    for c, after in zip(copies_in, copies_out, strict=True):
        c.wait()
        after.start()
    for c in copies_out:
        c.wait()


def results(width):
    items = [((ROPE, width), BF16), ((width // LANES, LANES), BF16)]
    items += [((OWN, ROPE), F32)] * 3 + [((1, OWN), F32)] * 3
    return [jax.ShapeDtypeStruct(s, t) for s, t in items]


def step(operands):
    hidden = operands[0]
    tokens, width = hidden.shape
    dma = pltpu.SemaphoreType.DMA
    piece = (SPAN, 16, LANES)
    others = NX * NY - 1
    chunk = (NEAR, *piece)
    counts = [NEAR, NEAR, 0, NEAR, NEAR, NEAR, FAR, FAR, NEAR, NEAR, 0, NEAR, 0, NEAR, FAR, FAR]
    return pl.pallas_call(
        step_kernel,
        out_shape=results(width),
        in_specs=[pl.BlockSpec(memory_space=pltpu.HBM)] * len(operands),
        out_specs=[pl.BlockSpec(memory_space=pltpu.HBM)] * 8,
        scratch_shapes=[
            pltpu.VMEM((NC, NEAR, NX, NY, *piece), BF16),
            pltpu.VMEM((ROPE, width), BF16),
            pltpu.VMEM((width // LANES, LANES), BF16),
        ]
        + [pltpu.VMEM(o.shape, o.dtype) for o in operands]
        + [
            pltpu.VMEM((2 * LANES, LANES), F32),
            pltpu.VMEM((SPAN, BLOCK, LANES), F32),
            pltpu.VMEM((8, 2 * LANES), jnp.int32),
            pltpu.VMEM((width // LANES, LANES), F32),
            pltpu.VMEM((NEAR, NC, NX, NY, *piece), BF16),
            pltpu.VMEM((16, LANES), F32),
            pltpu.VMEM((NEAR, NX, NY, *piece), BF16),
            pltpu.VMEM((NEAR, NX, NY, *piece), BF16),
            pltpu.VMEM((NEAR, others, *piece), BF16),
            pltpu.VMEM(chunk, BF16),
            pltpu.VMEM(chunk, BF16),
            pltpu.VMEM(piece, BF16),
            pltpu.VMEM((FAR, *piece), BF16),
            pltpu.VMEM((16, LANES), BF16),
            pltpu.VMEM((FAR, 16, LANES), BF16),
            pltpu.VMEM((3, *piece), F32),
            pltpu.VMEM(piece, F32),
            dma((len(operands) - 1,)),
            dma((tokens // ROWS,)),
            pltpu.SemaphoreType.REGULAR((2,)),
            dma((6 + NZL + 1,)),
        ]
        + [dma((n,)) if n else dma for n in counts],
        compiler_params=pltpu.CompilerParams(
            collective_id=0, has_side_effects=True, vmem_limit_bytes=56 * 1024 * 1024
        ),
    )(*operands)


def hand_on(arrays):
    hbm = [pl.BlockSpec(memory_space=pltpu.HBM)] * len(arrays)
    copies = arrays[0].shape[0] // 16 + len(arrays) - 1
    return pl.pallas_call(
        functools.partial(copy_kernel, len(arrays)),
        out_shape=[jax.ShapeDtypeStruct(a.shape, a.dtype) for a in arrays],
        in_specs=hbm,
        out_specs=hbm,
        scratch_shapes=[pltpu.VMEM(a.shape, a.dtype) for a in arrays]
        + [pltpu.SemaphoreType.DMA((copies,))] * 2,
        compiler_params=pltpu.CompilerParams(vmem_limit_bytes=56 * 1024 * 1024),
    )(*arrays)


def shards(
    hidden, segment_ids, key_grad, weight_bf16, gain_bf16,
    weight_master, weight_first, weight_second, gain_master, gain_first, gain_second,
):
    width = hidden.shape[1]
    states = [weight_master, weight_first, weight_second]
    states += [g.reshape(1, OWN) for g in (gain_master, gain_first, gain_second)]
    operands = [hidden, segment_ids, key_grad.T, weight_bf16.T, gain_bf16.reshape(width // LANES, LANES)]
    arrays = step([*operands, jnp.asarray(rotary_table()), *states])
    weight_t, gain, wm, wf, ws, gm, gf, gs = hand_on(arrays)
    return (
        wm, wf, ws, gm.reshape(OWN), gf.reshape(OWN), gs.reshape(OWN), weight_t.T, gain.reshape(width)
    )


def solution(mesh):
    both = P(("outer", "inner"), None)
    one = P(("outer", "inner"))
    return jax.shard_map(
        shards,
        mesh=mesh,
        in_specs=(both, both, both, P(), P(), both, both, both, one, one, one),
        out_specs=(both, both, both, one, one, one, P(), P()),
        check_vma=False,
    )
```
